32 devices in a mesh: gx: 2 (over x), gy: 8 (over z, y), gz: 2 (over core).
Axes of the slice: x: 2, y: 2, z: 4, core: 2. Of those that a mesh axis runs over, the one named last changes fastest.
Arguments:
- tensor: float32 [64, 256, 512], P('gx', 'gy', 'gz'), may hold values from -6 to 6
- core: float32 [256, 256, 128], P('gx', 'gy', 'gz'), may hold values from -6 to 6
- factor_one: float32 [64, 256], P('gx'), may hold values from -0.375 to 0.375
- factor_two: float32 [256, 256], P('gy'), may hold values from -0.375 to 0.375
- factor_three: float32 [512, 128], P('gz'), may hold values from -0.5 to 0.5
Outputs:
- residual: float32 [64, 256, 512], P('gx', 'gy', 'gz')
- grad_one: float32 [64, 256], P('gx')
- grad_two: float32 [256, 256], P('gy')
- grad_three: float32 [512, 128], P('gz')
The draws below stay inside these ranges and needn't reach their ends.
All inputs are finite; a program needn't handle non-finite values.
Results may differ from the reference program's by a relative error of at most 0.00007.
Values sent between devices are 32-bit elements; how exact they have to be, the bound alone decides.
No kernel may reach another device: no remote copies, remote signals or barrier semaphores. Data moves between devices by JAX's collectives and lax.ppermute only.
A program may use at most 64 MiB of HBM per device.

```python
import jax
import jax.numpy as jnp
from jax import lax

R1 = 256
R2 = 256
R3 = 128
I1 = 64
I2 = 256
I3 = 512


def block_scale(rng, extent, cuts, least, high):
    loudness, own = 1.0, jax.random.fold_in(rng, 6)
    for position, blocks in cuts:
        steps = jnp.exp(jax.random.uniform(jax.random.fold_in(own, position), (blocks,), jnp.float32, least / len(cuts), high / len(cuts)))
        loudness = loudness * jnp.repeat(steps, extent[position] // blocks).reshape([-1 if axis == position else 1 for axis in range(len(extent))])
    return loudness


def normal_values(rng, extent, width, reach, pieces=(), kind=jnp.bfloat16):
    array = jax.random.normal(rng, extent, jnp.float32) * width
    if len(pieces) > 0:
        array = block_scale(rng, extent, pieces, -0.22, 0.18) * array
    return jnp.clip(array, min=-reach, max=reach).astype(kind)


def setup_inputs(seed: int = 0) -> dict:
    key_list = jax.random.split(jax.random.key(seed), 6)
    tensor = normal_values(key_list[0], (I1, I2, I3), 1.0, 6.0, ((0, 2), (1, 8), (2, 2)), jnp.float32)
    core = normal_values(key_list[1], (R1, R2, R3), 1.0, 6.0, ((0, 2), (1, 8), (2, 2)), jnp.float32)
    factor_one = normal_values(key_list[2], (I1, R1), R1 ** -0.5, 0.375, ((0, 2),), jnp.float32)
    factor_two = normal_values(key_list[3], (I2, R2), R2 ** -0.5, 0.375, ((0, 8),), jnp.float32)
    factor_three = normal_values(key_list[4], (I3, R3), R3 ** -0.5, 0.5, ((0, 2),), jnp.float32)
    return {"tensor": tensor, "core": core, "factor_one": factor_one, "factor_two": factor_two, "factor_three": factor_three}


highest = lax.Precision.HIGHEST

def reference(tensor, core, factor_one, factor_two, factor_three):
    after_one = jnp.einsum('ir,rst->ist', factor_one, core, precision=highest)
    after_two = jnp.einsum('js,ist->ijt', factor_two, after_one, precision=highest)
    approx = jnp.einsum('ijt,kt->ijk', after_two, factor_three, precision=highest)
    residual = approx - tensor
    folded = jnp.einsum('ijk,kt->ijt', residual, factor_three, precision=highest)
    wide_one = jnp.einsum('ijt,js->ist', folded, factor_two, precision=highest)
    grad_one = jnp.einsum('ist,rst->ir', wide_one, core, precision=highest)
    wide_two = jnp.einsum('ijt,ir->rjt', folded, factor_one, precision=highest)
    grad_two = jnp.einsum('rjt,rst->js', wide_two, core, precision=highest)
    grad_three = jnp.einsum('ijk,ijt->kt', residual, after_two, precision=highest)
    grad_one = grad_one / jnp.sqrt(jnp.float32(I2 * I3))
    grad_two = grad_two / jnp.sqrt(jnp.float32(I1 * I3))
    grad_three = grad_three / jnp.sqrt(jnp.float32(I1 * I2))
    return (residual, grad_one, grad_two, grad_three)
```

```python
import jax
import jax.numpy as jnp
from jax import lax
from jax.sharding import PartitionSpec as P

highest = lax.Precision.HIGHEST


def dot(spec, left, right):
    return jnp.einsum(spec, left, right, precision=highest)


def swap(x, axis):
    return lax.ppermute(x, axis, [(0, 1), (1, 0)])


def part(x, index):
    return lax.dynamic_index_in_dim(x, index, 0, keepdims=False)


def in_order(axis, mine, other):
    first = lax.axis_index(axis) == 0
    return jnp.stack([jnp.where(first, mine, other), jnp.where(first, other, mine)])


def trade(x, axis):
    if lax.axis_size(axis) != 2:
        return lax.all_to_all(x, axis, 0, 0, tiled=True)
    me = lax.axis_index(axis)
    return in_order(axis, part(x, me), swap(part(x, 1 - me), axis))


def gather(x, axis):
    if lax.axis_size(axis) != 2:
        return lax.all_gather(x, axis)
    return in_order(axis, x, swap(x, axis))


def reduce_scatter(x, axis):
    if lax.axis_size(axis) != 2:
        return lax.psum_scatter(x, axis, scatter_dimension=0)
    me = lax.axis_index(axis)
    return part(x, me) + swap(part(x, 1 - me), axis)


def total(x, axis):
    if lax.axis_size(axis) != 2:
        return lax.psum(x, axis)
    return x + swap(x, axis)


def local(tensor, core, factor_one, factor_two, factor_three):
    nx, ny, nz = lax.axis_size("gx"), lax.axis_size("gy"), lax.axis_size("gz")
    i, j, k = tensor.shape
    r, s, t = core.shape
    e, q, full_t, full_s, full_r = i // (ny * nz), s // nz, t * nz, s * ny, r * nx
    half_j, half_s = j // nz, full_s // nz

    own = trade(core.reshape(r, nz, q, t).transpose(1, 0, 2, 3), "gz")
    own = own.transpose(1, 2, 0, 3).reshape(r, q, full_t)
    rows = trade(factor_one.reshape(i, nx, r).transpose(1, 0, 2), "gx").reshape(nx * i, r)

    folded_tensor = dot("abc,ct->abt", tensor, factor_three)
    folded_tensor = reduce_scatter(folded_tensor.reshape(nz, ny, e * j, full_t), "gz")
    mine_two = part(factor_two.reshape(nz, half_j, full_s), lax.axis_index("gz"))
    mine_two = mine_two.reshape(half_j, ny, nz, q).transpose(2, 0, 1, 3).reshape(nz * half_j, half_s)
    early = jnp.concatenate(
        [folded_tensor, jnp.broadcast_to(mine_two.reshape(1, -1, full_t), (ny, nz * half_j * half_s // full_t, full_t))],
        axis=1,
    )
    early = lax.all_to_all(early, "gy", 0, 0, tiled=True)
    folded_tensor = early[:, : e * j].reshape(ny, e, j, full_t).transpose(1, 0, 2, 3).reshape(e, ny * j, full_t)
    all_two = gather(early[:, e * j :].reshape(ny, nz, half_j, half_s), "gz")
    all_two = all_two.transpose(1, 0, 3, 2, 4).reshape(ny * j, full_s)
    gram = total(dot("ct,cu->tu", factor_three, factor_three), "gz")

    after_one = dot("ar,rst->ast", rows, own).reshape(nx, i, q, full_t)
    after_one = reduce_scatter(after_one, "gx").reshape(nz * ny, e, q, full_t)
    after_one = lax.all_to_all(after_one, ("gz", "gy"), 0, 0, tiled=True)
    after_one = after_one.transpose(1, 0, 2, 3).reshape(e, full_s, full_t)

    after_two = dot("bs,ast->abt", all_two, after_one)
    moved = after_two.reshape(e, ny, j, full_t).transpose(1, 0, 2, 3)
    moved = lax.all_to_all(moved, "gy", 0, 0, tiled=True).reshape(ny * e, j, full_t)

    folded = dot("abt,tu->abu", after_two, gram) - folded_tensor
    wide_one = dot("abt,bs->ast", folded, all_two)
    term_two = dot("abt,ast->bs", folded, after_one)

    after_full = gather(moved, "gz").reshape(i, j, full_t)
    residual = dot("abt,ct->abc", after_full, factor_three) - tensor
    term_three = dot("abc,abt->ct", residual, after_full)

    late = jnp.concatenate(
        [
            wide_one.reshape(e, nz * ny, q, full_t).transpose(1, 0, 2, 3).reshape(nz * ny, e * q, full_t),
            term_two.reshape(ny, j, nz, half_s).transpose(2, 0, 1, 3).reshape(nz * ny, -1, full_t),
            term_three.reshape(ny, nz, -1, full_t).transpose(1, 0, 2, 3).reshape(nz * ny, -1, full_t),
        ],
        axis=1,
    )
    late = lax.all_to_all(late, ("gz", "gy"), 0, 0, tiled=True)
    edge_one, edge_two = e * q, e * q + j * half_s // full_t
    share_one = late[:, :edge_one].reshape(i, q, full_t)
    share_two = late[:, edge_one:edge_two].sum(axis=0)
    share_three = late[:, edge_two:].reshape(nz, ny, -1, full_t).sum(axis=1)
    every_core = gather(own, "gx")
    term_one = dot("ast,xrst->axr", share_one, every_core).reshape(i, nz, full_r // nz).transpose(1, 0, 2)
    term_one = reduce_scatter(term_one, "gz")

    share_two = total(share_two, "gx").reshape(j, half_s)
    share_three = total(share_three, "gx")
    share_three = trade(share_three, "gz").reshape(-1, full_t)
    grad_two = gather(share_two, "gz").reshape(nz, j, ny, q).transpose(1, 2, 0, 3).reshape(j, full_s)

    last = jnp.concatenate([term_one.reshape(-1, full_t), share_three], axis=0)
    last = lax.all_to_all(jnp.broadcast_to(last[None], (ny,) + last.shape), "gy", 0, 0, tiled=True)
    rows_one = i * (full_r // nz) // full_t
    grad_one = last[:, :rows_one].sum(axis=0).reshape(i, full_r // nz)
    grad_one = gather(grad_one, "gz").transpose(1, 0, 2).reshape(i, full_r)
    grad_three = last[:, rows_one:].reshape(k, full_t)

    grad_one = grad_one / jnp.sqrt(jnp.float32(j * ny * k * nz))
    grad_two = grad_two / jnp.sqrt(jnp.float32(i * nx * k * nz))
    grad_three = grad_three / jnp.sqrt(jnp.float32(i * nx * j * ny))
    return (residual, grad_one, grad_two, grad_three)


def solution(mesh):
    placed = (P("gx", "gy", "gz"), P("gx", "gy", "gz"), P("gx", None), P("gy", None), P("gz", None))
    return jax.shard_map(
        local,
        mesh=mesh,
        in_specs=placed,
        out_specs=(P("gx", "gy", "gz"), P("gx", None), P("gy", None), P("gz", None)),
        check_vma=False,
    )
```

```python
import jax
import jax.numpy as jnp
from jax import lax
from jax.experimental import pallas as pl
from jax.experimental.pallas import tpu as pltpu
from jax.sharding import PartitionSpec as P

highest = lax.Precision.HIGHEST


def dot(spec, left, right):
    return jnp.einsum(spec, left, right, precision=highest)


def swap(x, axis):
    return lax.ppermute(x, axis, [(0, 1), (1, 0)])


def part(x, index):
    return lax.dynamic_index_in_dim(x, index, 0, keepdims=False)


def in_order(axis, mine, other):
    first = lax.axis_index(axis) == 0
    return jnp.stack([jnp.where(first, mine, other), jnp.where(first, other, mine)])


def trade(x, axis):
    if lax.axis_size(axis) != 2:
        return lax.all_to_all(x, axis, 0, 0, tiled=True)
    me = lax.axis_index(axis)
    return in_order(axis, part(x, me), swap(part(x, 1 - me), axis))


def gather(x, axis):
    if lax.axis_size(axis) != 2:
        return lax.all_gather(x, axis)
    return in_order(axis, x, swap(x, axis))


def reduce_scatter(x, axis):
    if lax.axis_size(axis) != 2:
        return lax.psum_scatter(x, axis, scatter_dimension=0)
    me = lax.axis_index(axis)
    return part(x, me) + swap(part(x, 1 - me), axis)


def total(x, axis):
    if lax.axis_size(axis) != 2:
        return lax.psum(x, axis)
    return x + swap(x, axis)


def fit(place, tensor, moved, factor_three, nz):
    i, j, k = tensor.shape
    full_t = moved.shape[1]
    if nz != 2:
        after_full = gather(moved, "gz").reshape(i * j, full_t)
        mine, other = after_full, after_full
    else:
        mine, other = moved, swap(moved, "gz")
    steps = 4
    block = i * j // steps
    each = mine.shape[0] // block

    def body(place_ref, tensor_ref, mine_ref, other_ref, factor_ref, residual_ref, sum_ref):
        step = pl.program_id(0)
        mine_here = step // each == place_ref[0]
        after = jnp.where(mine_here, mine_ref[...], other_ref[...])
        left = (
            lax.dot_general(after, factor_ref[...], (((1,), (1,)), ((), ())), precision=highest, preferred_element_type=jnp.float32)
            - tensor_ref[...]
        )
        residual_ref[...] = left
        term = lax.dot_general(left, after, (((0,), (0,)), ((), ())), precision=highest, preferred_element_type=jnp.float32)

        @pl.when(step == 0)
        def _():
            sum_ref[...] = term

        @pl.when(step > 0)
        def _():
            sum_ref[...] += term

    residual, term = pl.pallas_call(
        body,
        grid_spec=pltpu.PrefetchScalarGridSpec(
            num_scalar_prefetch=1,
            grid=(steps,),
            in_specs=[
                pl.BlockSpec((block, k), lambda n, place: (n, 0)),
                pl.BlockSpec((block, full_t), lambda n, place: (n % each, 0)),
                pl.BlockSpec((block, full_t), lambda n, place: (n % each, 0)),
                pl.BlockSpec((k, full_t), lambda n, place: (0, 0)),
            ],
            out_specs=[
                pl.BlockSpec((block, k), lambda n, place: (n, 0)),
                pl.BlockSpec((k, full_t), lambda n, place: (0, 0)),
            ],
        ),
        out_shape=[jax.ShapeDtypeStruct((i * j, k), jnp.float32), jax.ShapeDtypeStruct((k, full_t), jnp.float32)],
        compiler_params=pltpu.CompilerParams(vmem_limit_bytes=32 * 1024 * 1024),
        cost_estimate=pl.CostEstimate(flops=24 * i * j * k * full_t, bytes_accessed=8 * i * j * k, transcendentals=0),
    )(place, tensor.reshape(i * j, k), mine, other, factor_three)
    return residual.reshape(i, j, k), term


def local(tensor, core, factor_one, factor_two, factor_three):
    nx, ny, nz = lax.axis_size("gx"), lax.axis_size("gy"), lax.axis_size("gz")
    i, j, k = tensor.shape
    r, s, t = core.shape
    e, q, full_t, full_s, full_r = i // (ny * nz), s // nz, t * nz, s * ny, r * nx
    half_j, half_s = j // nz, full_s // nz

    own = trade(core.reshape(r, nz, q, t).transpose(1, 0, 2, 3), "gz")
    own = own.transpose(1, 2, 0, 3).reshape(r, q, full_t)
    rows = trade(factor_one.reshape(i, nx, r).transpose(1, 0, 2), "gx").reshape(nx * i, r)

    rows_last = lax.axis_index("gz").reshape(1).astype(jnp.int32)

    folded_tensor = dot("abc,ct->abt", tensor, factor_three).reshape(i, nz, half_j, full_t)
    folded_tensor = reduce_scatter(folded_tensor.transpose(1, 0, 2, 3), "gz").reshape(nz * ny, e * half_j, full_t)
    gram = total(dot("ct,cu->tu", factor_three, factor_three), "gz")

    after_one = dot("ar,rst->ast", rows, own).reshape(nx, i, q, full_t)
    after_one = reduce_scatter(after_one, "gx").reshape(nz * ny, e * q, full_t)

    mine_two = part(factor_two.reshape(nz, half_j, full_s), lax.axis_index("gz"))
    mine_two = mine_two.reshape(half_j, ny, nz, q).transpose(2, 0, 1, 3).reshape(1, -1, full_t)
    mine_two = jnp.broadcast_to(mine_two, (nz * ny,) + mine_two.shape[1:])
    early = jnp.concatenate([after_one, folded_tensor, mine_two], axis=1)
    early = lax.all_to_all(early, ("gz", "gy"), 0, 0, tiled=True)
    cut, cut_two = e * q, e * q + e * half_j
    after_one = early[:, :cut].reshape(nz * ny, e, q, full_t).transpose(1, 0, 2, 3).reshape(e, full_s, full_t)
    folded_tensor = early[:, cut:cut_two].reshape(nz, ny, e, half_j, full_t).transpose(2, 1, 0, 3, 4).reshape(e, ny * j, full_t)
    all_two = early[:, cut_two:].reshape(nz, ny, nz, half_j, half_s).transpose(1, 0, 3, 2, 4).reshape(ny * j, full_s)

    after_two = dot("bs,ast->abt", all_two, after_one)
    moved = after_two.reshape(e, ny, j, full_t).transpose(1, 0, 2, 3)
    moved = lax.all_to_all(moved, "gy", 0, 0, tiled=True).reshape(ny * e * j, full_t)

    folded = dot("abt,tu->abu", after_two, gram) - folded_tensor
    wide_one = dot("abt,bs->ast", folded, all_two)
    term_two = dot("abt,ast->bs", folded, after_one).reshape(ny * j, nz, half_s)
    term_two = reduce_scatter(term_two.transpose(1, 0, 2), "gz")

    residual, term_three = fit(rows_last, tensor, moved, factor_three, nz)

    late = jnp.concatenate(
        [
            wide_one.reshape(e, nz * ny, q, full_t).transpose(1, 0, 2, 3).reshape(nz * ny, e * q, full_t),
            term_two.reshape(ny, nz, -1, full_t).transpose(1, 0, 2, 3).reshape(nz * ny, -1, full_t),
            term_three.reshape(ny, nz, -1, full_t).transpose(1, 0, 2, 3).reshape(nz * ny, -1, full_t),
        ],
        axis=1,
    )
    late = lax.all_to_all(late, ("gz", "gy"), 0, 0, tiled=True)
    cut = e * q
    share_one = late[:, :cut].reshape(i, q, full_t)
    sums = total(late[:, cut:].reshape(nz, ny, -1, full_t).sum(axis=1), "gx")
    cut = half_j * half_s // full_t
    share_two, share_three = sums[:, :cut], sums[:, cut:]
    every_core = gather(own, "gx")
    term_one = dot("ast,xrst->axr", share_one, every_core).reshape(i, nz, full_r // nz).transpose(1, 0, 2)
    term_one = reduce_scatter(term_one, "gz")

    share_two = share_two.reshape(nz, half_j, ny, q).transpose(1, 2, 0, 3).reshape(half_j, full_s)
    grad_two = gather(share_two, "gz").reshape(j, full_s)

    last = jnp.concatenate([term_one.reshape(nz, -1, full_t), share_three], axis=1)
    last = jnp.broadcast_to(last[:, None], (nz, ny) + last.shape[1:])
    last = lax.all_to_all(last.reshape((nz * ny,) + last.shape[2:]), ("gz", "gy"), 0, 0, tiled=True)
    last = last.reshape((nz, ny) + last.shape[1:])
    cut = (i // nz) * (full_r // nz) // full_t
    grad_one = last[:, :, :cut].sum(axis=1).reshape(nz, i // nz, full_r // nz)
    grad_one = gather(grad_one.transpose(1, 0, 2).reshape(i // nz, full_r), "gz").reshape(i, full_r)
    grad_three = last[:, :, cut:].transpose(1, 0, 2, 3).reshape(k, full_t)

    grad_one = grad_one / jnp.sqrt(jnp.float32(j * ny * k * nz))
    grad_two = grad_two / jnp.sqrt(jnp.float32(i * nx * k * nz))
    grad_three = grad_three / jnp.sqrt(jnp.float32(i * nx * j * ny))
    return (residual, grad_one, grad_two, grad_three)


def solution(mesh):
    placed = (P("gx", "gy", "gz"), P("gx", "gy", "gz"), P("gx", None), P("gy", None), P("gz", None))
    return jax.shard_map(
        local,
        mesh=mesh,
        in_specs=placed,
        out_specs=(P("gx", "gy", "gz"), P("gx", None), P("gy", None), P("gz", None)),
        check_vma=False,
    )
```

```python
import jax
import jax.numpy as jnp
from jax import lax
from jax.experimental import pallas as pl
from jax.experimental.pallas import tpu as pltpu
from jax.sharding import PartitionSpec as P

highest = lax.Precision.HIGHEST
f32 = jnp.float32
vmem = pl.BlockSpec(memory_space=pltpu.VMEM)
hbm = pl.BlockSpec(memory_space=pl.ANY)
smem = pl.BlockSpec(memory_space=pltpu.SMEM)
params = pltpu.CompilerParams(vmem_limit_bytes=14 * 1024 * 1024)


def shape(*sizes):
    return jax.ShapeDtypeStruct(sizes, f32)


def dot(spec, left, right):
    return jnp.einsum(spec, left, right, precision=highest)


def product(left, right, dims):
    return lax.dot_general(left, right, (dims, ((), ())), precision=highest, preferred_element_type=f32)


def swap(x, axis):
    return lax.ppermute(x, axis, [(0, 1), (1, 0)])


def part(x, index):
    return lax.dynamic_index_in_dim(x, index, 0, keepdims=False)


def in_order(axis, mine, other):
    first = lax.axis_index(axis) == 0
    return jnp.stack([jnp.where(first, mine, other), jnp.where(first, other, mine)])


def trade(x, axis):
    if lax.axis_size(axis) != 2:
        return lax.all_to_all(x, axis, 0, 0, tiled=True)
    me = lax.axis_index(axis)
    return in_order(axis, part(x, me), swap(part(x, 1 - me), axis))


def gather(x, axis):
    if lax.axis_size(axis) != 2:
        return lax.all_gather(x, axis)
    return in_order(axis, x, swap(x, axis))


def total(x, axis):
    if lax.axis_size(axis) != 2:
        return lax.psum(x, axis)
    return x + swap(x, axis)


def mode_one(rows, core):
    a, s, t = rows.shape[0], core.shape[0], core.shape[1]
    halves = 128 // t
    q = s // halves

    def body(rows_ref, core_ref, out_ref):
        left = rows_ref[...]
        for n in range(q):
            right = jnp.concatenate([core_ref[h * q + n] for h in range(halves)], axis=0)
            out_ref[:, n, :] = product(left, right, ((1,), (1,)))

    return pl.pallas_call(
        body,
        out_shape=shape(a, q, halves * t),
        in_specs=[vmem, vmem],
        out_specs=vmem,
        compiler_params=params,
        cost_estimate=pl.CostEstimate(flops=12 * a * s * t * 128, bytes_accessed=4 * s * t * 128, transcendentals=0),
    )(rows, core)


def mode_two(place, arrived, mine, other, e, t):
    nz, ny, rows, wide = arrived.shape
    q, halves, half_j, full_s = rows // e, wide // t, mine.shape[2], mine.shape[1] * wide
    j = nz * half_j

    def body(place_ref, arrived_ref, mine_ref, other_ref, one_ref, two_ref, moved_ref):
        me = place_ref[0]
        for c in range(mine_ref.shape[1]):
            here = pl.ds(c * wide, wide)
            two_ref[:, pl.ds(me, 1), :, here] = mine_ref[:, c][:, None]
            two_ref[:, pl.ds(1 - me, 1), :, here] = other_ref[:, c][:, None]
        for n in range(e):
            for h in range(halves):
                pieces = [arrived_ref[z, :, pl.ds(n * q, q), pl.ds(h * t, t)] for z in range(nz)]
                one_ref[:, h, :, pl.ds(n * wide, wide)] = jnp.concatenate(pieces, axis=-1)
        after = product(
            two_ref[...].reshape(ny * j, full_s), one_ref[...].reshape(full_s, e * wide), ((1,), (0,))
        )
        for n in range(e):
            moved_ref[:, n] = after[:, n * wide : (n + 1) * wide].reshape(ny, j, wide)

    one, two = (ny, halves, q, e * wide), (ny, nz, half_j, full_s)
    return pl.pallas_call(
        body,
        out_shape=[shape(*one), shape(*two), shape(ny, e, j, wide)],
        in_specs=[smem, vmem, vmem, vmem],
        out_specs=[vmem] * 3,
        compiler_params=params,
    )(place, arrived, mine, other)


def back(place, moved, gram, gram_other, early, one, two):
    ny, e, j, wide = moved.shape
    _, halves, q, _ = one.shape
    _, nz, half_j, full_s = two.shape

    def body(place_ref, moved_ref, gram_ref, gram_other_ref, early_ref, one_ref, two_ref, wide_ref, keep_ref, send_ref, sum_ref):
        me = place_ref[0]
        square = gram_ref[...] + gram_other_ref[...]
        whole_two = two_ref[...].reshape(ny * j, full_s)
        for n in range(e):
            folded = product(moved_ref[:, n].reshape(ny * j, wide), square, ((1,), (0,)))
            folded = folded - early_ref[:, pl.ds(n * j, j)].reshape(ny * j, wide)
            term = product(folded, one_ref[:, :, :, pl.ds(n * wide, wide)].reshape(full_s, wide), ((1,), (1,)))
            term = term.reshape(ny, nz, half_j, full_s)
            if n == 0:
                sum_ref[...] = term
            else:
                sum_ref[...] += term
            spread = product(whole_two, folded, ((0,), (0,))).reshape(ny, halves, q, wide)
            for h in range(halves):
                wide_ref[h, :, pl.ds(n * q, q)] = spread[:, h]
        keep_ref[...] = sum_ref[:, pl.ds(me, 1)].reshape(ny, half_j, full_s)
        send_ref[...] = sum_ref[:, pl.ds(1 - me, 1)].reshape(ny, half_j, full_s)

    return pl.pallas_call(
        body,
        out_shape=[shape(halves, ny, e * q, wide), shape(ny, half_j, full_s), shape(ny, half_j, full_s)],
        in_specs=[smem] + [vmem] * 6,
        out_specs=[vmem] * 3,
        scratch_shapes=[pltpu.VMEM((ny, nz, half_j, full_s), f32)],
        compiler_params=params,
        cost_estimate=pl.CostEstimate(flops=10**9, bytes_accessed=2**21, transcendentals=0),
    )(place, moved, gram, gram_other, early, one, two)


def fit(place, tensor, mine, other, factor_three, wide_one, keep, arrived):
    rows, k = tensor.shape
    block, full_t = mine.shape
    nz, ny, edge, _ = wide_one.shape
    half_j = keep.shape[1]
    cut = k // (ny * nz)

    def body(place_ref, tensor_ref, mine_ref, other_ref, factor_ref, wide_ref, keep_ref, arrived_ref, residual_ref, late_ref, field_ref, left_ref, sems):
        me = place_ref[0]
        at = [pl.ds(pl.multiple_of(h * block, block), block) for h in (me, 1 - me)]
        fields = [pltpu.make_async_copy(tensor_ref.at[at[h]], field_ref.at[h], sems.at[h]) for h in range(2)]
        lefts = [pltpu.make_async_copy(left_ref.at[h], residual_ref.at[at[h]], sems.at[2 + h]) for h in range(2)]
        wide = pltpu.make_async_copy(wide_ref, late_ref.at[:, :, pl.ds(0, edge)], sems.at[4])
        for copy in fields:
            copy.start()
        wide.start()
        both = keep_ref[...] + arrived_ref[...]
        for z in range(nz):
            late_ref[z, :, pl.ds(edge, half_j)] = both[:, :, z * full_t : (z + 1) * full_t]
        term = jnp.zeros((full_t, k), f32)
        factor = factor_ref[...].T
        for h, ref in enumerate((mine_ref, other_ref)):
            after = ref[...]
            left = product(after, factor, ((1,), (0,)))
            fields[h].wait()
            left = left - field_ref[h]
            left_ref[h] = left
            lefts[h].start()
            term = term + product(after, left, ((0,), (0,)))
        pieces = term.T.reshape(ny, nz, cut, full_t)
        for z in range(nz):
            late_ref[z, :, pl.ds(edge + half_j, cut)] = pieces[:, z]
        wide.wait()
        for copy in lefts:
            copy.wait()

    return pl.pallas_call(
        body,
        out_shape=[shape(rows, k), shape(nz, ny, edge + half_j + cut, full_t)],
        in_specs=[smem, hbm, vmem, vmem, vmem, hbm, vmem, vmem],
        out_specs=[hbm, vmem],
        scratch_shapes=[pltpu.VMEM((2, block, k), f32), pltpu.VMEM((2, block, k), f32), pltpu.SemaphoreType.DMA((5,))],
        compiler_params=params,
        cost_estimate=pl.CostEstimate(flops=24 * rows * k * full_t, bytes_accessed=8 * rows * k, transcendentals=0),
    )(place, tensor, mine, other, factor_three, wide_one, keep, arrived)


def mode_one_term(place, late, own_mine, own_other, near_mine, near_other, e):
    n, _, wide = late.shape
    q, t, r = own_mine.shape
    i = n * e
    group = min(q, 256 // t)

    def body(place_ref, late_ref, own_mine_ref, own_other_ref, near_mine_ref, near_other_ref, keep_ref, send_ref, rows_ref):
        rows_ref[...] = late_ref[:, pl.ds(0, e * q)].reshape(i * q, wide)
        first = place_ref[0] == 0
        sum_here = jnp.zeros((i, 2 * r), f32)
        for p in range(0, q, group):
            parts = [rows_ref[pl.ds(p + m, i, stride=q), :] for m in range(group)]
            low = jnp.concatenate([x[:, :t] for x in parts], axis=1)
            high = jnp.concatenate([x[:, t:] for x in parts], axis=1)
            for left, pair in (
                (jnp.where(first, low, high), (own_mine_ref, near_mine_ref)),
                (jnp.where(first, high, low), (own_other_ref, near_other_ref)),
            ):
                right = jnp.concatenate([ref[pl.ds(p, group)].reshape(group * t, r) for ref in pair], axis=1)
                sum_here = sum_here + product(left, right, ((1,), (0,)))
        same = place_ref[0] == place_ref[1]
        keep_ref[...] = jnp.where(same, sum_here[:, :r], sum_here[:, r:])
        send_ref[...] = jnp.where(same, sum_here[:, r:], sum_here[:, :r])

    return pl.pallas_call(
        body,
        out_shape=[shape(i, r), shape(i, r)],
        in_specs=[smem] + [vmem] * 5,
        out_specs=[vmem] * 2,
        scratch_shapes=[pltpu.VMEM((i * q, wide), f32)],
        compiler_params=params,
    )(place, late, own_mine, own_other, near_mine, near_other)


def local(tensor, core, factor_one, factor_two, factor_three):
    nx, ny, nz = lax.axis_size("gx"), lax.axis_size("gy"), lax.axis_size("gz")
    i, j, k = tensor.shape
    r, s, t = core.shape
    e, q, full_t, full_s, full_r = i // (ny * nz), s // nz, t * nz, s * ny, r * nx
    half_j, half_r, rows = j // nz, full_r // nz, i * j
    gx, gz = lax.axis_index("gx"), lax.axis_index("gz")
    place = jnp.stack([gz, gx]).astype(jnp.int32)
    flat = core.transpose(1, 2, 0)

    if nx == 2:
        other_one = swap(lax.dynamic_slice_in_dim(factor_one, (1 - gx) * r, r, axis=1), "gx")

    halves = tensor.reshape(nz, rows // nz, k)
    folded = swap(dot("ac,ct->at", part(halves, 1 - gz), factor_three), "gz")
    folded = folded + dot("ac,ct->at", part(halves, gz), factor_three)
    mine_two = part(factor_two.reshape(nz, half_j, full_s), gz)
    mine_two = jnp.concatenate([mine_two[:, c * full_t : (c + 1) * full_t] for c in range(full_s // full_t)], axis=0)
    early = jnp.concatenate(
        [folded.reshape(ny, e * j, full_t), jnp.broadcast_to(mine_two[None], (ny,) + mine_two.shape)], axis=1
    )
    if nx == 2:
        mine_one = lax.dynamic_slice_in_dim(factor_one, gx * r, r, axis=1)
        early, other_one = lax.optimization_barrier((early, other_one))
        sent = swap(mode_one(other_one, flat), "gx")
        after_one = mode_one(mine_one, flat) + sent
    else:
        every_one = trade(factor_one.reshape(i, nx, r).transpose(1, 0, 2), "gx")
        after_one = dot("xar,hqtr->xaqht", every_one, flat.reshape(nz, q, t, r)).reshape(nx, i, q, full_t)
        after_one = lax.psum_scatter(after_one, "gx", scatter_dimension=0)

    early = lax.all_to_all(early, "gy", 0, 0, tiled=True)
    early, after_one = lax.optimization_barrier((early, after_one))
    mine_two = early[:, e * j :].reshape(ny, full_s // full_t, half_j, full_t)
    other_two = swap(mine_two, "gz")
    gram = dot("ct,cu->tu", factor_three, factor_three)
    gram_other = swap(gram, "gz")

    flat = flat.reshape(nz, q, t, r)
    if nx == 2:
        own_mine, own_other = part(flat, gz), swap(part(flat, 1 - gz), "gz")
        near_mine = swap(own_mine, "gx")
    after_one = lax.all_to_all(after_one.reshape(nz * ny, e * q, full_t), ("gz", "gy"), 0, 0, tiled=True)
    after_one = after_one.reshape(nz, ny, e * q, full_t)
    one, two, moved = mode_two(place, after_one, mine_two, other_two, e, t)
    home = lax.all_to_all(moved, "gy", 0, 0, tiled=True).reshape(rows // nz, full_t)
    wide_one, keep, send = back(place, moved, gram, gram_other, early, one, two)
    arrived = swap(send, "gz")

    home, arrived = lax.optimization_barrier((home, arrived))

    residual, late = fit(place, tensor.reshape(rows, k), home, swap(home, "gz"), factor_three, wide_one, keep, arrived)
    if nx == 2:
        late, near_mine = lax.optimization_barrier((late, near_mine))
    late = lax.all_to_all(late.reshape((nz * ny,) + late.shape[2:]), ("gz", "gy"), 0, 0, tiled=True)
    sums = total(late[:, e * q :].reshape(nz, ny, -1, full_t).sum(axis=1), "gx")
    share_two, share_three = sums[:, :half_j], sums[:, half_j:]
    if nx == 2:
        keep_one, send_one = mode_one_term(place, late, own_mine, own_other, near_mine, swap(own_other, "gx"), e)
        term_one = keep_one + swap(send_one, "gz")
    else:
        share_one = late[:, : e * q].reshape(i, q, full_t)
        every_core = gather(trade(flat, "gz"), "gx")
        term_one = dot("aqht,xhqtr->axr", share_one.reshape(i, q, nz, t), every_core)
        term_one = lax.psum_scatter(term_one.reshape(i, nz, half_r).transpose(1, 0, 2), "gz", scatter_dimension=0)

    last = jnp.concatenate([term_one.reshape(nz, -1, full_t), share_three], axis=1)
    last = jnp.broadcast_to(last[:, None], (nz, ny) + last.shape[1:])
    last = lax.all_to_all(last.reshape((nz * ny,) + last.shape[2:]), ("gz", "gy"), 0, 0, tiled=True)
    last = last.reshape((nz, ny) + last.shape[1:])
    cut = (i // nz) * half_r // full_t
    grad_one = last[:, :, :cut].sum(axis=1).reshape(nz, i // nz, half_r)
    grad_one = gather(grad_one.transpose(1, 0, 2).reshape(i // nz, full_r), "gz").reshape(i, full_r)
    grad_three = last[:, :, cut:].transpose(1, 0, 2, 3).reshape(k, full_t)
    share_two = gather(share_two.reshape(j, full_s // nz), "gz")
    grad_two = jnp.concatenate([share_two[z] for z in range(nz)], axis=1)

    grad_one = grad_one / jnp.sqrt(f32(j * ny * k * nz))
    grad_two = grad_two / jnp.sqrt(f32(i * nx * k * nz))
    grad_three = grad_three / jnp.sqrt(f32(i * nx * j * ny))
    return (residual.reshape(i, j, k), grad_one, grad_two, grad_three)


def solution(mesh):
    placed = (P("gx", "gy", "gz"), P("gx", "gy", "gz"), P("gx", None), P("gy", None), P("gz", None))
    return jax.shard_map(
        local,
        mesh=mesh,
        in_specs=placed,
        out_specs=(P("gx", "gy", "gz"), P("gx", None), P("gy", None), P("gz", None)),
        check_vma=False,
    )
```

```python
import jax
import jax.numpy as jnp
from jax import lax
from jax.experimental import pallas as pl
from jax.experimental.pallas import tpu as pltpu
from jax.sharding import PartitionSpec as P

highest = lax.Precision.HIGHEST
f32 = jnp.float32
vmem = pl.BlockSpec(memory_space=pltpu.VMEM)
hbm = pl.BlockSpec(memory_space=pl.ANY)
smem = pl.BlockSpec(memory_space=pltpu.SMEM)
params = pltpu.CompilerParams(vmem_limit_bytes=14 * 1024 * 1024)


def shape(*sizes):
    return jax.ShapeDtypeStruct(sizes, f32)


def dot(spec, left, right):
    return jnp.einsum(spec, left, right, precision=highest)


def product(left, right, dims):
    return lax.dot_general(left, right, (dims, ((), ())), precision=highest, preferred_element_type=f32)


def swap(x, axis):
    return lax.ppermute(x, axis, [(0, 1), (1, 0)])


def part(x, index):
    return lax.dynamic_index_in_dim(x, index, 0, keepdims=False)


def in_order(axis, mine, other):
    first = lax.axis_index(axis) == 0
    return jnp.stack([jnp.where(first, mine, other), jnp.where(first, other, mine)])


def trade(x, axis):
    if lax.axis_size(axis) != 2:
        return lax.all_to_all(x, axis, 0, 0, tiled=True)
    me = lax.axis_index(axis)
    return in_order(axis, part(x, me), swap(part(x, 1 - me), axis))


def gather(x, axis):
    if lax.axis_size(axis) != 2:
        return lax.all_gather(x, axis)
    return in_order(axis, x, swap(x, axis))


def total(x, axis):
    if lax.axis_size(axis) != 2:
        return lax.psum(x, axis)
    return x + swap(x, axis)


def fold_tensor(half, tensor, factor_three):
    rows, k = tensor.shape
    block, full_t = rows // 2, factor_three.shape[1]
    pieces = 2
    cut = block // pieces

    def body(half_ref, tensor_ref, factor_in, keep_ref, send_ref, copy_ref, field_ref, whole_ref, factor_ref, loads_sem, stores_sem, sem):
        me = half_ref[0]
        weight = pltpu.make_async_copy(factor_in, factor_ref, sem)
        weight.start()
        ats = [pl.ds(n * cut, cut) for n in range(2 * pieces)]
        loads = [pltpu.make_async_copy(tensor_ref.at[at], field_ref.at[at], loads_sem.at[n]) for n, at in enumerate(ats)]
        stores = [pltpu.make_async_copy(field_ref.at[at], copy_ref.at[at], stores_sem.at[n]) for n, at in enumerate(ats)]
        for copy in loads:
            copy.start()
        for n in range(2 * pieces):
            loads[n].wait()
            stores[n].start()
        weight.wait()
        whole_ref[...] = product(field_ref[...], factor_ref[...], ((1,), (0,)))
        keep_ref[...] = whole_ref[pl.ds(pl.multiple_of(me * block, block), block), :]
        send_ref[...] = whole_ref[pl.ds(pl.multiple_of((1 - me) * block, block), block), :]
        for copy in stores:
            copy.wait()

    dma = pltpu.SemaphoreType.DMA
    return pl.pallas_call(
        body,
        out_shape=[shape(block, full_t), shape(block, full_t), shape(rows, k)],
        in_specs=[smem, hbm, hbm],
        out_specs=[vmem, vmem, hbm],
        scratch_shapes=[
            pltpu.VMEM((rows, k), f32),
            pltpu.VMEM((rows, full_t), f32),
            pltpu.VMEM(factor_three.shape, f32),
            dma((2 * pieces,)),
            dma((2 * pieces,)),
            dma,
        ],
        compiler_params=pltpu.CompilerParams(vmem_limit_bytes=63 * 1024 * 1024),
    )(half, tensor, factor_three)


def pack_early(half, keep, arrived, factor_two, ny, nz):
    j, full_s = factor_two.shape
    wide = keep.shape[1]
    edge, half_j = keep.shape[0] // ny, j // nz
    parts = full_s // wide

    def body(half_ref, keep_ref, arrived_ref, factor_ref, out_ref, rows_ref, sem):
        at = pl.ds(pl.multiple_of(half_ref[0] * half_j, half_j), half_j)
        copy = pltpu.make_async_copy(factor_ref.at[at], rows_ref, sem)
        copy.start()
        out_ref[:, pl.ds(0, edge)] = (keep_ref[...] + arrived_ref[...]).reshape(ny, edge, wide)
        copy.wait()
        for c in range(parts):
            piece = rows_ref[:, c * wide : (c + 1) * wide]
            out_ref[:, pl.ds(edge + c * half_j, half_j)] = jnp.broadcast_to(piece[None], (ny, half_j, wide))

    return pl.pallas_call(
        body,
        out_shape=shape(ny, edge + parts * half_j, wide),
        in_specs=[smem, vmem, vmem, hbm],
        out_specs=vmem,
        scratch_shapes=[pltpu.VMEM((half_j, full_s), f32), pltpu.SemaphoreType.DMA],
        compiler_params=params,
    )(half, keep, arrived, factor_two)


def mode_one(rows, core):
    a, s, t = rows.shape[0], core.shape[0], core.shape[1]
    halves = 128 // t
    q = s // halves

    def body(rows_ref, core_ref, out_ref):
        left = rows_ref[...]
        for n in range(q):
            right = jnp.concatenate([core_ref[h * q + n] for h in range(halves)], axis=0)
            out_ref[:, n, :] = product(left, right, ((1,), (1,)))

    return pl.pallas_call(
        body,
        out_shape=shape(a, q, halves * t),
        in_specs=[vmem, vmem],
        out_specs=vmem,
        compiler_params=params,
        cost_estimate=pl.CostEstimate(flops=12 * a * s * t * 128, bytes_accessed=4 * s * t * 128, transcendentals=0),
    )(rows, core)


def mode_two(place, arrived, mine, other, e, t):
    nz, ny, rows, wide = arrived.shape
    q, halves, half_j, full_s = rows // e, wide // t, mine.shape[2], mine.shape[1] * wide
    j = nz * half_j

    def body(place_ref, arrived_ref, mine_ref, other_ref, one_ref, two_ref, moved_ref):
        me = place_ref[0]
        for c in range(mine_ref.shape[1]):
            here = pl.ds(c * wide, wide)
            two_ref[:, pl.ds(me, 1), :, here] = mine_ref[:, c][:, None]
            two_ref[:, pl.ds(1 - me, 1), :, here] = other_ref[:, c][:, None]
        for n in range(e):
            for h in range(halves):
                pieces = [arrived_ref[z, :, pl.ds(n * q, q), pl.ds(h * t, t)] for z in range(nz)]
                one_ref[:, h, :, pl.ds(n * wide, wide)] = jnp.concatenate(pieces, axis=-1)
        after = product(
            two_ref[...].reshape(ny * j, full_s), one_ref[...].reshape(full_s, e * wide), ((1,), (0,))
        )
        for n in range(e):
            moved_ref[:, n] = after[:, n * wide : (n + 1) * wide].reshape(ny, j, wide)

    one, two = (ny, halves, q, e * wide), (ny, nz, half_j, full_s)
    return pl.pallas_call(
        body,
        out_shape=[shape(*one), shape(*two), shape(ny, e, j, wide)],
        in_specs=[smem, vmem, vmem, vmem],
        out_specs=[vmem] * 3,
        compiler_params=params,
    )(place, arrived, mine, other)


def back(place, moved, gram, gram_other, early, one, two, length):
    ny, e, j, wide = moved.shape
    _, halves, q, _ = one.shape
    _, nz, half_j, full_s = two.shape

    def body(place_ref, moved_ref, gram_ref, gram_other_ref, early_ref, one_ref, two_ref, late_ref, keep_ref, send_ref, sum_ref, wide_ref, sem):
        me = place_ref[0]
        square = gram_ref[...] + gram_other_ref[...]
        whole_two = two_ref[...].reshape(ny * j, full_s)
        for n in range(e):
            folded = product(moved_ref[:, n].reshape(ny * j, wide), square, ((1,), (0,)))
            folded = folded - early_ref[:, pl.ds(n * j, j)].reshape(ny * j, wide)
            term = product(folded, one_ref[:, :, :, pl.ds(n * wide, wide)].reshape(full_s, wide), ((1,), (1,)))
            term = term.reshape(ny, nz, half_j, full_s)
            if n == 0:
                sum_ref[...] = term
            else:
                sum_ref[...] += term
            spread = product(whole_two, folded, ((0,), (0,))).reshape(ny, halves, q, wide)
            for h in range(halves):
                wide_ref[h, :, pl.ds(n * q, q)] = spread[:, h]
        copy = pltpu.make_async_copy(wide_ref, late_ref.at[:, :, pl.ds(0, e * q)], sem)
        copy.start()
        keep_ref[...] = sum_ref[:, pl.ds(me, 1)].reshape(ny, half_j, full_s)
        send_ref[...] = sum_ref[:, pl.ds(1 - me, 1)].reshape(ny, half_j, full_s)
        copy.wait()

    return pl.pallas_call(
        body,
        out_shape=[shape(halves, ny, length, wide), shape(ny, half_j, full_s), shape(ny, half_j, full_s)],
        in_specs=[smem] + [vmem] * 6,
        out_specs=[hbm, vmem, vmem],
        scratch_shapes=[
            pltpu.VMEM((ny, nz, half_j, full_s), f32),
            pltpu.VMEM((halves, ny, e * q, wide), f32),
            pltpu.SemaphoreType.DMA,
        ],
        compiler_params=params,
        cost_estimate=pl.CostEstimate(flops=10**9, bytes_accessed=2**21, transcendentals=0),
    )(place, moved, gram, gram_other, early, one, two)


def put_two(late, keep, arrived, edge):
    nz, ny, _, wide = late.shape
    half_j = keep.shape[1]

    def body(_, keep_ref, arrived_ref, late_ref, both_ref, sem):
        both = keep_ref[...] + arrived_ref[...]
        for z in range(nz):
            both_ref[z] = both[:, :, z * wide : (z + 1) * wide]
        copy = pltpu.make_async_copy(both_ref, late_ref.at[:, :, pl.ds(edge, half_j)], sem)
        copy.start()
        copy.wait()

    return pl.pallas_call(
        body,
        out_shape=shape(*late.shape),
        in_specs=[hbm, vmem, vmem],
        out_specs=hbm,
        scratch_shapes=[pltpu.VMEM((nz, ny, half_j, wide), f32), pltpu.SemaphoreType.DMA],
        input_output_aliases={0: 0},
        compiler_params=params,
    )(late, keep, arrived)


def fit(half, field, after, factor_three, before=None):
    rows, k = field.shape
    block, full_t = after.shape

    def compute(half_ref, after_ref, factor_ref, residual_ref, field_ref, left_ref, sems):
        at = pl.ds(pl.multiple_of(half_ref[0] * block, block), block)
        field = pltpu.make_async_copy(residual_ref.at[at], field_ref, sems.at[0])
        field.start()
        after = after_ref[...]
        left = product(after, factor_ref[...].T, ((1,), (0,)))
        field.wait()
        left = left - field_ref[...]
        left_ref[...] = left
        out = pltpu.make_async_copy(left_ref, residual_ref.at[at], sems.at[1])
        out.start()
        return product(after, left, ((0,), (0,))), out

    scratch = [pltpu.VMEM((block, k), f32), pltpu.VMEM((block, k), f32), pltpu.SemaphoreType.DMA((3,))]
    if before is None:

        def body(half_ref, _, after_ref, factor_ref, residual_ref, term_ref, field_ref, left_ref, sems):
            term, out = compute(half_ref, after_ref, factor_ref, residual_ref, field_ref, left_ref, sems)
            term_ref[...] = term
            out.wait()

        return pl.pallas_call(
            body,
            out_shape=[shape(rows, k), shape(full_t, k)],
            in_specs=[smem, hbm, vmem, vmem],
            out_specs=[hbm, vmem],
            scratch_shapes=scratch,
            input_output_aliases={1: 0},
            compiler_params=params,
        )(half, field, after, factor_three)

    term, late = before
    nz, ny, length, _ = late.shape
    cut = k // (ny * nz)

    def body(half_ref, _, after_ref, factor_ref, term_ref, __, residual_ref, late_ref, field_ref, left_ref, sems, pieces_ref):
        term, out = compute(half_ref, after_ref, factor_ref, residual_ref, field_ref, left_ref, sems)
        pieces = (term + term_ref[...]).T.reshape(ny, nz, cut, full_t)
        for z in range(nz):
            pieces_ref[z] = pieces[:, z]
        copy = pltpu.make_async_copy(pieces_ref, late_ref.at[:, :, pl.ds(length - cut, cut)], sems.at[2])
        copy.start()
        copy.wait()
        out.wait()

    return pl.pallas_call(
        body,
        out_shape=[shape(rows, k), shape(*late.shape)],
        in_specs=[smem, hbm, vmem, vmem, vmem, hbm],
        out_specs=[hbm, hbm],
        scratch_shapes=scratch + [pltpu.VMEM((nz, ny, cut, full_t), f32)],
        input_output_aliases={1: 0, 5: 1},
        compiler_params=params,
    )(half, field, after, factor_three, term, late)


def mode_one_term(place, late, own_mine, own_other, near_mine, near_other, e):
    n, _, wide = late.shape
    q, t, r = own_mine.shape
    i = n * e
    group = min(q, 256 // t)

    def body(place_ref, late_ref, own_mine_ref, own_other_ref, near_mine_ref, near_other_ref, keep_ref, send_ref, rows_ref):
        rows_ref[...] = late_ref[:, pl.ds(0, e * q)].reshape(i * q, wide)
        first = place_ref[0] == 0
        sum_here = jnp.zeros((i, 2 * r), f32)
        for p in range(0, q, group):
            parts = [rows_ref[pl.ds(p + m, i, stride=q), :] for m in range(group)]
            low = jnp.concatenate([x[:, :t] for x in parts], axis=1)
            high = jnp.concatenate([x[:, t:] for x in parts], axis=1)
            for left, pair in (
                (jnp.where(first, low, high), (own_mine_ref, near_mine_ref)),
                (jnp.where(first, high, low), (own_other_ref, near_other_ref)),
            ):
                right = jnp.concatenate([ref[pl.ds(p, group)].reshape(group * t, r) for ref in pair], axis=1)
                sum_here = sum_here + product(left, right, ((1,), (0,)))
        same = place_ref[0] == place_ref[1]
        keep_ref[...] = jnp.where(same, sum_here[:, :r], sum_here[:, r:])
        send_ref[...] = jnp.where(same, sum_here[:, r:], sum_here[:, :r])

    return pl.pallas_call(
        body,
        out_shape=[shape(i, r), shape(i, r)],
        in_specs=[smem] + [vmem] * 5,
        out_specs=[vmem] * 2,
        scratch_shapes=[pltpu.VMEM((i * q, wide), f32)],
        compiler_params=params,
    )(place, late, own_mine, own_other, near_mine, near_other)


def local(tensor, core, factor_one, factor_two, factor_three):
    nx, ny, nz = lax.axis_size("gx"), lax.axis_size("gy"), lax.axis_size("gz")
    i, j, k = tensor.shape
    r, s, t = core.shape
    e, q, full_t, full_s, full_r = i // (ny * nz), s // nz, t * nz, s * ny, r * nx
    half_j, half_r, rows = j // nz, full_r // nz, i * j
    gx, gz = lax.axis_index("gx"), lax.axis_index("gz")
    place = jnp.stack([gz, gx]).astype(jnp.int32)
    flat = core.transpose(1, 2, 0)

    if nx == 2:
        other_one = swap(lax.dynamic_slice_in_dim(factor_one, (1 - gx) * r, r, axis=1), "gx")

    half = place[:1]
    keep, send, field = fold_tensor(half, tensor.reshape(rows, k), factor_three)
    early = pack_early(half, keep, swap(send, "gz"), factor_two, ny, nz)
    if nx == 2:
        mine_one = lax.dynamic_slice_in_dim(factor_one, gx * r, r, axis=1)
        early, other_one = lax.optimization_barrier((early, other_one))
        sent = swap(mode_one(other_one, flat), "gx")
        after_one = mode_one(mine_one, flat) + sent
    else:
        every_one = trade(factor_one.reshape(i, nx, r).transpose(1, 0, 2), "gx")
        after_one = dot("xar,hqtr->xaqht", every_one, flat.reshape(nz, q, t, r)).reshape(nx, i, q, full_t)
        after_one = lax.psum_scatter(after_one, "gx", scatter_dimension=0)

    early = lax.all_to_all(early, "gy", 0, 0, tiled=True)
    early, after_one = lax.optimization_barrier((early, after_one))
    mine_two = early[:, e * j :].reshape(ny, full_s // full_t, half_j, full_t)
    other_two = swap(mine_two, "gz")
    gram = dot("ct,cu->tu", factor_three, factor_three)
    gram_other = swap(gram, "gz")

    flat = flat.reshape(nz, q, t, r)
    if nx == 2:
        own_mine, own_other = part(flat, gz), swap(part(flat, 1 - gz), "gz")
        near_mine = swap(own_mine, "gx")
    after_one = lax.all_to_all(after_one.reshape(nz * ny, e * q, full_t), ("gz", "gy"), 0, 0, tiled=True)
    after_one = after_one.reshape(nz, ny, e * q, full_t)
    one, two, moved = mode_two(place, after_one, mine_two, other_two, e, t)
    home = lax.all_to_all(moved, "gy", 0, 0, tiled=True).reshape(rows // nz, full_t)
    late, keep, send = back(place, moved, gram, gram_other, early, one, two, e * q + half_j + k // (ny * nz))
    late = put_two(late, keep, swap(send, "gz"), e * q)

    if nx == 2:
        home, late, near_mine = lax.optimization_barrier((home, late, near_mine))

    field, term_three = fit(half, field, home, factor_three)
    residual, late = fit(1 - half, field, swap(home, "gz"), factor_three, (term_three, late))
    late = lax.all_to_all(late.reshape((nz * ny,) + late.shape[2:]), ("gz", "gy"), 0, 0, tiled=True)
    sums = total(late[:, e * q :].reshape(nz, ny, -1, full_t).sum(axis=1), "gx")
    share_two, share_three = sums[:, :half_j], sums[:, half_j:]
    if nx == 2:
        keep_one, send_one = mode_one_term(place, late, own_mine, own_other, near_mine, swap(own_other, "gx"), e)
        term_one = keep_one + swap(send_one, "gz")
    else:
        share_one = late[:, : e * q].reshape(i, q, full_t)
        every_core = gather(trade(flat, "gz"), "gx")
        term_one = dot("aqht,xhqtr->axr", share_one.reshape(i, q, nz, t), every_core)
        term_one = lax.psum_scatter(term_one.reshape(i, nz, half_r).transpose(1, 0, 2), "gz", scatter_dimension=0)

    last = jnp.concatenate([term_one.reshape(nz, -1, full_t), share_three], axis=1)
    last = jnp.broadcast_to(last[:, None], (nz, ny) + last.shape[1:])
    last = lax.all_to_all(last.reshape((nz * ny,) + last.shape[2:]), ("gz", "gy"), 0, 0, tiled=True)
    last = last.reshape((nz, ny) + last.shape[1:])
    cut = (i // nz) * half_r // full_t
    grad_one = last[:, :, :cut].sum(axis=1).reshape(nz, i // nz, half_r)
    grad_one = gather(grad_one.transpose(1, 0, 2).reshape(i // nz, full_r), "gz").reshape(i, full_r)
    grad_three = last[:, :, cut:].transpose(1, 0, 2, 3).reshape(k, full_t)
    share_two = gather(share_two.reshape(j, full_s // nz), "gz")
    grad_two = jnp.concatenate([share_two[z] for z in range(nz)], axis=1)

    grad_one = grad_one / jnp.sqrt(f32(j * ny * k * nz))
    grad_two = grad_two / jnp.sqrt(f32(i * nx * k * nz))
    grad_three = grad_three / jnp.sqrt(f32(i * nx * j * ny))
    return (residual.reshape(i, j, k), grad_one, grad_two, grad_three)


def solution(mesh):
    placed = (P("gx", "gy", "gz"), P("gx", "gy", "gz"), P("gx", None), P("gy", None), P("gz", None))
    return jax.shard_map(
        local,
        mesh=mesh,
        in_specs=placed,
        out_specs=(P("gx", "gy", "gz"), P("gx", None), P("gy", None), P("gz", None)),
        check_vma=False,
    )
```

```python
import jax
import jax.numpy as jnp
from jax import lax
from jax.experimental import pallas as pl
from jax.experimental.pallas import tpu as pltpu
from jax.sharding import PartitionSpec as P

highest = lax.Precision.HIGHEST
f32 = jnp.float32
vmem = pl.BlockSpec(memory_space=pltpu.VMEM)
hbm = pl.BlockSpec(memory_space=pl.ANY)
smem = pl.BlockSpec(memory_space=pltpu.SMEM)
params = pltpu.CompilerParams(vmem_limit_bytes=14 * 1024 * 1024)


def shape(*sizes):
    return jax.ShapeDtypeStruct(sizes, f32)


def dot(spec, left, right):
    return jnp.einsum(spec, left, right, precision=highest)


def product(left, right, dims):
    return lax.dot_general(left, right, (dims, ((), ())), precision=highest, preferred_element_type=f32)


def swap(x, axis):
    return lax.ppermute(x, axis, [(0, 1), (1, 0)])


def part(x, index):
    return lax.dynamic_index_in_dim(x, index, 0, keepdims=False)


def in_order(axis, mine, other):
    first = lax.axis_index(axis) == 0
    return jnp.stack([jnp.where(first, mine, other), jnp.where(first, other, mine)])


def trade(x, axis):
    if lax.axis_size(axis) != 2:
        return lax.all_to_all(x, axis, 0, 0, tiled=True)
    me = lax.axis_index(axis)
    return in_order(axis, part(x, me), swap(part(x, 1 - me), axis))


def gather(x, axis):
    if lax.axis_size(axis) != 2:
        return lax.all_gather(x, axis)
    return in_order(axis, x, swap(x, axis))


def total(x, axis):
    if lax.axis_size(axis) != 2:
        return lax.psum(x, axis)
    return x + swap(x, axis)


def mode_one(rows, core):
    a, s, t = rows.shape[0], core.shape[0], core.shape[1]
    halves = 128 // t
    q = s // halves

    def body(rows_ref, core_ref, out_ref):
        right = jnp.concatenate([core_ref[h * q + n] for n in range(q) for h in range(halves)], axis=0)
        both = product(rows_ref[...], right, ((1,), (1,)))
        for n in range(q):
            out_ref[:, n, :] = both[:, n * halves * t : (n + 1) * halves * t]

    return pl.pallas_call(
        body,
        out_shape=shape(a, q, halves * t),
        in_specs=[vmem, vmem],
        out_specs=vmem,
        compiler_params=params,
        cost_estimate=pl.CostEstimate(flops=12 * a * s * t * 128, bytes_accessed=4 * s * t * 128, transcendentals=0),
    )(rows, core)


def mode_two(place, arrived, mine, other, e, t):
    nz, ny, rows, wide = arrived.shape
    q, halves, half_j, full_s = rows // e, wide // t, mine.shape[2], mine.shape[1] * wide
    j = nz * half_j

    def body(place_ref, arrived_ref, mine_ref, other_ref, one_ref, two_ref, moved_ref):
        me = place_ref[0]
        for c in range(mine_ref.shape[1]):
            here = pl.ds(c * wide, wide)
            two_ref[:, pl.ds(me, 1), :, here] = mine_ref[:, c][:, None]
            two_ref[:, pl.ds(1 - me, 1), :, here] = other_ref[:, c][:, None]
        for n in range(e):
            for h in range(halves):
                pieces = [arrived_ref[z, :, pl.ds(n * q, q), pl.ds(h * t, t)] for z in range(nz)]
                one_ref[:, h, :, pl.ds(n * wide, wide)] = jnp.concatenate(pieces, axis=-1)
        after = product(
            two_ref[...].reshape(ny * j, full_s), one_ref[...].reshape(full_s, e * wide), ((1,), (0,))
        )
        for n in range(e):
            moved_ref[:, n] = after[:, n * wide : (n + 1) * wide].reshape(ny, j, wide)

    one, two = (ny, halves, q, e * wide), (ny, nz, half_j, full_s)
    return pl.pallas_call(
        body,
        out_shape=[shape(*one), shape(*two), shape(ny, e, j, wide)],
        in_specs=[smem, vmem, vmem, vmem],
        out_specs=[vmem] * 3,
        compiler_params=params,
    )(place, arrived, mine, other)


def back(place, moved, gram, gram_other, early, one, two, length):
    ny, e, j, wide = moved.shape
    _, halves, q, _ = one.shape
    _, nz, half_j, full_s = two.shape

    def body(place_ref, moved_ref, gram_ref, gram_other_ref, early_ref, one_ref, two_ref, late_ref, keep_ref, send_ref, sum_ref, wide_ref, sem):
        me = place_ref[0]
        square = gram_ref[...] + gram_other_ref[...]
        whole_two = two_ref[...].reshape(ny * j, full_s)
        for n in range(e):
            folded = product(moved_ref[:, n].reshape(ny * j, wide), square, ((1,), (0,)))
            folded = folded - early_ref[:, pl.ds(n * j, j)].reshape(ny * j, wide)
            term = product(folded, one_ref[:, :, :, pl.ds(n * wide, wide)].reshape(full_s, wide), ((1,), (1,)))
            term = term.reshape(ny, nz, half_j, full_s)
            if n == 0:
                sum_ref[...] = term
            else:
                sum_ref[...] += term
            spread = product(whole_two, folded, ((0,), (0,))).reshape(ny, halves, q, wide)
            for h in range(halves):
                wide_ref[h, :, pl.ds(n * q, q)] = spread[:, h]
        copy = pltpu.make_async_copy(wide_ref, late_ref.at[:, :, pl.ds(0, e * q)], sem)
        copy.start()
        keep_ref[...] = sum_ref[:, pl.ds(me, 1)].reshape(ny, half_j, full_s)
        send_ref[...] = sum_ref[:, pl.ds(1 - me, 1)].reshape(ny, half_j, full_s)
        copy.wait()

    return pl.pallas_call(
        body,
        out_shape=[shape(halves, ny, length, wide), shape(ny, half_j, full_s), shape(ny, half_j, full_s)],
        in_specs=[smem] + [vmem] * 6,
        out_specs=[hbm, vmem, vmem],
        scratch_shapes=[
            pltpu.VMEM((ny, nz, half_j, full_s), f32),
            pltpu.VMEM((halves, ny, e * q, wide), f32),
            pltpu.SemaphoreType.DMA,
        ],
        compiler_params=params,
        cost_estimate=pl.CostEstimate(flops=10**9, bytes_accessed=2**21, transcendentals=0),
    )(place, moved, gram, gram_other, early, one, two)


def put_two(late, keep, arrived, edge):
    nz, ny, _, wide = late.shape
    half_j = keep.shape[1]

    def body(_, keep_ref, arrived_ref, late_ref, both_ref, sem):
        both = keep_ref[...] + arrived_ref[...]
        for z in range(nz):
            both_ref[z] = both[:, :, z * wide : (z + 1) * wide]
        copy = pltpu.make_async_copy(both_ref, late_ref.at[:, :, pl.ds(edge, half_j)], sem)
        copy.start()
        copy.wait()

    return pl.pallas_call(
        body,
        out_shape=shape(*late.shape),
        in_specs=[hbm, vmem, vmem],
        out_specs=hbm,
        scratch_shapes=[pltpu.VMEM((nz, ny, half_j, wide), f32), pltpu.SemaphoreType.DMA],
        input_output_aliases={0: 0},
        compiler_params=params,
    )(late, keep, arrived)


def fit(half, field, after, factor_three, before=None):
    rows, k = field.shape
    block, full_t = after.shape
    pieces = 1

    def compute(half_ref, after_ref, factor_ref, residual_ref, field_ref, left_ref, sems):
        cut = block // pieces
        ats = [pl.ds(pl.multiple_of(half_ref[0] * block + n * cut, cut), cut) for n in range(pieces)]
        here = [pl.ds(n * cut, cut) for n in range(pieces)]
        loads = [pltpu.make_async_copy(residual_ref.at[ats[n]], field_ref.at[here[n]], sems.at[n]) for n in range(pieces)]
        outs = [pltpu.make_async_copy(left_ref.at[here[n]], residual_ref.at[ats[n]], sems.at[pieces + n]) for n in range(pieces)]
        for copy in loads:
            copy.start()
        after = after_ref[...]
        left = product(after, factor_ref[...].T, ((1,), (0,)))
        for copy in loads:
            copy.wait()
        left = left - field_ref[...]
        left_ref[...] = left
        for copy in outs:
            copy.start()
        return product(after, left, ((0,), (0,))), outs

    scratch = [pltpu.VMEM((block, k), f32), pltpu.VMEM((block, k), f32), pltpu.SemaphoreType.DMA((2 * pieces + 1,))]
    if before is None:

        def body(half_ref, _, after_ref, factor_ref, residual_ref, term_ref, field_ref, left_ref, sems):
            term, outs = compute(half_ref, after_ref, factor_ref, residual_ref, field_ref, left_ref, sems)
            term_ref[...] = term
            for copy in outs:
                copy.wait()

        return pl.pallas_call(
            body,
            out_shape=[shape(rows, k), shape(full_t, k)],
            in_specs=[smem, hbm, vmem, vmem],
            out_specs=[hbm, vmem],
            scratch_shapes=scratch,
            input_output_aliases={1: 0},
            compiler_params=params,
        )(half, field, after, factor_three)

    term, late = before
    nz, ny, length, _ = late.shape
    cut = k // (ny * nz)

    def body(half_ref, _, after_ref, factor_ref, term_ref, __, residual_ref, late_ref, field_ref, left_ref, sems, parted_ref):
        term, outs = compute(half_ref, after_ref, factor_ref, residual_ref, field_ref, left_ref, sems)
        parted = (term + term_ref[...]).T.reshape(ny, nz, cut, full_t)
        for z in range(nz):
            parted_ref[z] = parted[:, z]
        message = pltpu.make_async_copy(parted_ref, late_ref.at[:, :, pl.ds(length - cut, cut)], sems.at[2 * pieces])
        message.start()
        for copy in outs:
            copy.wait()
        message.wait()

    return pl.pallas_call(
        body,
        out_shape=[shape(rows, k), shape(*late.shape)],
        in_specs=[smem, hbm, vmem, vmem, vmem, hbm],
        out_specs=[hbm, hbm],
        scratch_shapes=scratch + [pltpu.VMEM((nz, ny, cut, full_t), f32)],
        input_output_aliases={1: 0, 5: 1},
        compiler_params=params,
    )(half, field, after, factor_three, term, late)


def mode_one_term(place, late, own_mine, own_other, near_mine, near_other, e):
    n, _, wide = late.shape
    q, t, r = own_mine.shape
    i = n * e
    group = min(q, 256 // t)

    def body(place_ref, late_ref, own_mine_ref, own_other_ref, near_mine_ref, near_other_ref, keep_ref, send_ref, rows_ref):
        rows_ref[...] = late_ref[:, pl.ds(0, e * q)].reshape(i * q, wide)
        first = place_ref[0] == 0
        sum_here = jnp.zeros((i, 2 * r), f32)
        for p in range(0, q, group):
            parts = [rows_ref[pl.ds(p + m, i, stride=q), :] for m in range(group)]
            low = jnp.concatenate([x[:, :t] for x in parts], axis=1)
            high = jnp.concatenate([x[:, t:] for x in parts], axis=1)
            for left, pair in (
                (jnp.where(first, low, high), (own_mine_ref, near_mine_ref)),
                (jnp.where(first, high, low), (own_other_ref, near_other_ref)),
            ):
                right = jnp.concatenate([ref[pl.ds(p, group)].reshape(group * t, r) for ref in pair], axis=1)
                sum_here = sum_here + product(left, right, ((1,), (0,)))
        same = place_ref[0] == place_ref[1]
        keep_ref[...] = jnp.where(same, sum_here[:, :r], sum_here[:, r:])
        send_ref[...] = jnp.where(same, sum_here[:, r:], sum_here[:, :r])

    return pl.pallas_call(
        body,
        out_shape=[shape(i, r), shape(i, r)],
        in_specs=[smem] + [vmem] * 5,
        out_specs=[vmem] * 2,
        scratch_shapes=[pltpu.VMEM((i * q, wide), f32)],
        compiler_params=params,
    )(place, late, own_mine, own_other, near_mine, near_other)


def local(tensor, core, factor_one, factor_two, factor_three):
    nx, ny, nz = lax.axis_size("gx"), lax.axis_size("gy"), lax.axis_size("gz")
    i, j, k = tensor.shape
    r, s, t = core.shape
    e, q, full_t, full_s, full_r = i // (ny * nz), s // nz, t * nz, s * ny, r * nx
    half_j, half_r, rows = j // nz, full_r // nz, i * j
    gx, gz = lax.axis_index("gx"), lax.axis_index("gz")
    place = jnp.stack([gz, gx]).astype(jnp.int32)
    flat = core.transpose(1, 2, 0)

    if nx == 2:
        other_one = swap(lax.dynamic_slice_in_dim(factor_one, (1 - gx) * r, r, axis=1), "gx")

    half = place[:1]
    field = tensor.reshape(rows, k)
    halves = tensor.reshape(nz, rows // nz, k)
    folded = swap(dot("ac,ct->at", part(halves, 1 - gz), factor_three), "gz")
    folded = folded + dot("ac,ct->at", part(halves, gz), factor_three)
    mine_two = part(factor_two.reshape(nz, half_j, full_s), gz)
    mine_two = jnp.concatenate([mine_two[:, c * full_t : (c + 1) * full_t] for c in range(full_s // full_t)], axis=0)
    early = jnp.concatenate(
        [folded.reshape(ny, e * j, full_t), jnp.broadcast_to(mine_two[None], (ny,) + mine_two.shape)], axis=1
    )
    if nx == 2:
        mine_one = lax.dynamic_slice_in_dim(factor_one, gx * r, r, axis=1)
        early, other_one = lax.optimization_barrier((early, other_one))
        sent = swap(mode_one(other_one, flat), "gx")
        after_one = mode_one(mine_one, flat) + sent
    else:
        every_one = trade(factor_one.reshape(i, nx, r).transpose(1, 0, 2), "gx")
        after_one = dot("xar,hqtr->xaqht", every_one, flat.reshape(nz, q, t, r)).reshape(nx, i, q, full_t)
        after_one = lax.psum_scatter(after_one, "gx", scatter_dimension=0)

    early = lax.all_to_all(early, "gy", 0, 0, tiled=True)
    early, after_one = lax.optimization_barrier((early, after_one))
    mine_two = early[:, e * j :].reshape(ny, full_s // full_t, half_j, full_t)
    other_two = swap(mine_two, "gz")
    gram = dot("ct,cu->tu", factor_three, factor_three)
    gram_other = swap(gram, "gz")

    flat = flat.reshape(nz, q, t, r)
    if nx == 2:
        own_mine, own_other = part(flat, gz), swap(part(flat, 1 - gz), "gz")
        near_mine = swap(own_mine, "gx")
    after_one = lax.all_to_all(after_one.reshape(nz * ny, e * q, full_t), ("gz", "gy"), 0, 0, tiled=True)
    after_one = after_one.reshape(nz, ny, e * q, full_t)
    one, two, moved = mode_two(place, after_one, mine_two, other_two, e, t)
    home = lax.all_to_all(moved, "gy", 0, 0, tiled=True).reshape(rows // nz, full_t)
    late, keep, send = back(place, moved, gram, gram_other, early, one, two, e * q + half_j + k // (ny * nz))
    late = put_two(late, keep, swap(send, "gz"), e * q)

    if nx == 2:
        home, late, near_mine = lax.optimization_barrier((home, late, near_mine))

    field, term_three = fit(half, field, home, factor_three)
    residual, late = fit(1 - half, field, swap(home, "gz"), factor_three, (term_three, late))
    late = lax.all_to_all(late.reshape((nz * ny,) + late.shape[2:]), ("gz", "gy"), 0, 0, tiled=True)
    sums = total(late[:, e * q :].reshape(nz, ny, -1, full_t).sum(axis=1), "gx")
    share_two, share_three = sums[:, :half_j], sums[:, half_j:]
    if nx == 2:
        keep_one, send_one = mode_one_term(place, late, own_mine, own_other, near_mine, swap(own_other, "gx"), e)
        term_one = keep_one + swap(send_one, "gz")
    else:
        share_one = late[:, : e * q].reshape(i, q, full_t)
        every_core = gather(trade(flat, "gz"), "gx")
        term_one = dot("aqht,xhqtr->axr", share_one.reshape(i, q, nz, t), every_core)
        term_one = lax.psum_scatter(term_one.reshape(i, nz, half_r).transpose(1, 0, 2), "gz", scatter_dimension=0)

    last = jnp.concatenate([term_one.reshape(nz, -1, full_t), share_three], axis=1)
    last = jnp.broadcast_to(last[:, None], (nz, ny) + last.shape[1:])
    last = lax.all_to_all(last.reshape((nz * ny,) + last.shape[2:]), ("gz", "gy"), 0, 0, tiled=True)
    last = last.reshape((nz, ny) + last.shape[1:])
    cut = (i // nz) * half_r // full_t
    grad_one = last[:, :, :cut].sum(axis=1).reshape(nz, i // nz, half_r)
    grad_one = gather(grad_one.transpose(1, 0, 2).reshape(i // nz, full_r), "gz").reshape(i, full_r)
    grad_three = last[:, :, cut:].transpose(1, 0, 2, 3).reshape(k, full_t)
    share_two = gather(share_two.reshape(j, full_s // nz), "gz")
    grad_two = jnp.concatenate([share_two[z] for z in range(nz)], axis=1)

    grad_one = grad_one / jnp.sqrt(f32(j * ny * k * nz))
    grad_two = grad_two / jnp.sqrt(f32(i * nx * k * nz))
    grad_three = grad_three / jnp.sqrt(f32(i * nx * j * ny))
    return (residual.reshape(i, j, k), grad_one, grad_two, grad_three)


def solution(mesh):
    placed = (P("gx", "gy", "gz"), P("gx", "gy", "gz"), P("gx", None), P("gy", None), P("gz", None))
    return jax.shard_map(
        local,
        mesh=mesh,
        in_specs=placed,
        out_specs=(P("gx", "gy", "gz"), P("gx", None), P("gy", None), P("gz", None)),
        check_vma=False,
    )
```

```python
import jax
import jax.numpy as jnp
from jax import lax
from jax.experimental import pallas as pl
from jax.experimental.pallas import tpu as pltpu
from jax.sharding import PartitionSpec as P

highest = lax.Precision.HIGHEST
f32 = jnp.float32
vmem = pl.BlockSpec(memory_space=pltpu.VMEM)
hbm = pl.BlockSpec(memory_space=pl.ANY)
smem = pl.BlockSpec(memory_space=pltpu.SMEM)
params = pltpu.CompilerParams(vmem_limit_bytes=14 * 1024 * 1024)


def shape(*sizes):
    return jax.ShapeDtypeStruct(sizes, f32)


def dot(spec, left, right):
    return jnp.einsum(spec, left, right, precision=highest)


def product(left, right, dims):
    return lax.dot_general(left, right, (dims, ((), ())), precision=highest, preferred_element_type=f32)


def swap(x, axis):
    return lax.ppermute(x, axis, [(0, 1), (1, 0)])


def part(x, index):
    return lax.dynamic_index_in_dim(x, index, 0, keepdims=False)


def in_order(axis, mine, other):
    first = lax.axis_index(axis) == 0
    return jnp.stack([jnp.where(first, mine, other), jnp.where(first, other, mine)])


def trade(x, axis):
    if lax.axis_size(axis) != 2:
        return lax.all_to_all(x, axis, 0, 0, tiled=True)
    me = lax.axis_index(axis)
    return in_order(axis, part(x, me), swap(part(x, 1 - me), axis))


def gather(x, axis):
    if lax.axis_size(axis) != 2:
        return lax.all_gather(x, axis)
    return in_order(axis, x, swap(x, axis))


def total(x, axis):
    if lax.axis_size(axis) != 2:
        return lax.psum(x, axis)
    return x + swap(x, axis)


def mode_one(rows, core):
    a, s, t = rows.shape[0], core.shape[0], core.shape[1]
    halves = 128 // t
    q = s // halves

    def body(rows_ref, core_ref, out_ref):
        right = jnp.concatenate([core_ref[h * q + n] for n in range(q) for h in range(halves)], axis=0)
        both = product(rows_ref[...], right, ((1,), (1,)))
        for n in range(q):
            out_ref[:, n, :] = both[:, n * halves * t : (n + 1) * halves * t]

    return pl.pallas_call(
        body,
        out_shape=shape(a, q, halves * t),
        in_specs=[vmem, vmem],
        out_specs=vmem,
        compiler_params=params,
        cost_estimate=pl.CostEstimate(flops=12 * a * s * t * 128, bytes_accessed=4 * s * t * 128, transcendentals=0),
    )(rows, core)


def mode_two(place, arrived, mine, other, e, t):
    nz, ny, rows, wide = arrived.shape
    q, halves, half_j, full_s = rows // e, wide // t, mine.shape[2], mine.shape[1] * wide
    j = nz * half_j

    def body(place_ref, arrived_ref, mine_ref, other_ref, one_ref, two_ref, moved_ref):
        me = place_ref[0]
        for c in range(mine_ref.shape[1]):
            here = pl.ds(c * wide, wide)
            two_ref[:, pl.ds(me, 1), :, here] = mine_ref[:, c][:, None]
            two_ref[:, pl.ds(1 - me, 1), :, here] = other_ref[:, c][:, None]
        for n in range(e):
            for h in range(halves):
                pieces = [arrived_ref[z, :, pl.ds(n * q, q), pl.ds(h * t, t)] for z in range(nz)]
                one_ref[:, h, :, pl.ds(n * wide, wide)] = jnp.concatenate(pieces, axis=-1)
        after = product(
            two_ref[...].reshape(ny * j, full_s), one_ref[...].reshape(full_s, e * wide), ((1,), (0,))
        )
        for n in range(e):
            moved_ref[:, n] = after[:, n * wide : (n + 1) * wide].reshape(ny, j, wide)

    one, two = (ny, halves, q, e * wide), (ny, nz, half_j, full_s)
    return pl.pallas_call(
        body,
        out_shape=[shape(*one), shape(*two), shape(ny, e, j, wide)],
        in_specs=[smem, vmem, vmem, vmem],
        out_specs=[vmem] * 3,
        compiler_params=params,
    )(place, arrived, mine, other)


def back(place, moved, gram, gram_other, early, one, two, length):
    ny, e, j, wide = moved.shape
    _, halves, q, _ = one.shape
    _, nz, half_j, full_s = two.shape

    def body(place_ref, moved_ref, gram_ref, gram_other_ref, early_ref, one_ref, two_ref, late_ref, keep_ref, send_ref, sum_ref, wide_ref, sem):
        me = place_ref[0]
        square = gram_ref[...] + gram_other_ref[...]
        whole_two = two_ref[...].reshape(ny * j, full_s)
        for n in range(e):
            folded = product(moved_ref[:, n].reshape(ny * j, wide), square, ((1,), (0,)))
            folded = folded - early_ref[:, pl.ds(n * j, j)].reshape(ny * j, wide)
            term = product(folded, one_ref[:, :, :, pl.ds(n * wide, wide)].reshape(full_s, wide), ((1,), (1,)))
            term = term.reshape(ny, nz, half_j, full_s)
            if n == 0:
                sum_ref[...] = term
            else:
                sum_ref[...] += term
            spread = product(whole_two, folded, ((0,), (0,))).reshape(ny, halves, q, wide)
            for h in range(halves):
                wide_ref[h, :, pl.ds(n * q, q)] = spread[:, h]
        copy = pltpu.make_async_copy(wide_ref, late_ref.at[:, :, pl.ds(0, e * q)], sem)
        copy.start()
        keep_ref[...] = sum_ref[:, pl.ds(me, 1)].reshape(ny, half_j, full_s)
        send_ref[...] = sum_ref[:, pl.ds(1 - me, 1)].reshape(ny, half_j, full_s)
        copy.wait()

    return pl.pallas_call(
        body,
        out_shape=[shape(halves, ny, length, wide), shape(ny, half_j, full_s), shape(ny, half_j, full_s)],
        in_specs=[smem] + [vmem] * 6,
        out_specs=[hbm, vmem, vmem],
        scratch_shapes=[
            pltpu.VMEM((ny, nz, half_j, full_s), f32),
            pltpu.VMEM((halves, ny, e * q, wide), f32),
            pltpu.SemaphoreType.DMA,
        ],
        compiler_params=params,
        cost_estimate=pl.CostEstimate(flops=10**9, bytes_accessed=2**21, transcendentals=0),
    )(place, moved, gram, gram_other, early, one, two)


def put_two(late, keep, arrived, edge):
    nz, ny, _, wide = late.shape
    half_j = keep.shape[1]

    def body(_, keep_ref, arrived_ref, late_ref, both_ref, sem):
        both = keep_ref[...] + arrived_ref[...]
        for z in range(nz):
            both_ref[z] = both[:, :, z * wide : (z + 1) * wide]
        copy = pltpu.make_async_copy(both_ref, late_ref.at[:, :, pl.ds(edge, half_j)], sem)
        copy.start()
        copy.wait()

    return pl.pallas_call(
        body,
        out_shape=shape(*late.shape),
        in_specs=[hbm, vmem, vmem],
        out_specs=hbm,
        scratch_shapes=[pltpu.VMEM((nz, ny, half_j, wide), f32), pltpu.SemaphoreType.DMA],
        input_output_aliases={0: 0},
        compiler_params=params,
    )(late, keep, arrived)


def fit(half, field, after, factor_three, before=None):
    rows, k = field.shape
    block, full_t = after.shape
    pieces = 1

    def compute(half_ref, after_ref, factor_ref, residual_ref, field_ref, left_ref, sems):
        cut = block // pieces
        ats = [pl.ds(pl.multiple_of(half_ref[0] * block + n * cut, cut), cut) for n in range(pieces)]
        here = [pl.ds(n * cut, cut) for n in range(pieces)]
        loads = [pltpu.make_async_copy(residual_ref.at[ats[n]], field_ref.at[here[n]], sems.at[n]) for n in range(pieces)]
        outs = [pltpu.make_async_copy(left_ref.at[here[n]], residual_ref.at[ats[n]], sems.at[pieces + n]) for n in range(pieces)]
        for copy in loads:
            copy.start()
        after = after_ref[...]
        left = product(after, factor_ref[...].T, ((1,), (0,)))
        for copy in loads:
            copy.wait()
        left = left - field_ref[...]
        left_ref[...] = left
        for copy in outs:
            copy.start()
        return product(after, left, ((0,), (0,))), outs

    scratch = [pltpu.VMEM((block, k), f32), pltpu.VMEM((block, k), f32), pltpu.SemaphoreType.DMA((2 * pieces + 1,))]
    if before is None:

        def body(half_ref, _, after_ref, factor_ref, residual_ref, term_ref, field_ref, left_ref, sems):
            term, outs = compute(half_ref, after_ref, factor_ref, residual_ref, field_ref, left_ref, sems)
            term_ref[...] = term
            for copy in outs:
                copy.wait()

        return pl.pallas_call(
            body,
            out_shape=[shape(rows, k), shape(full_t, k)],
            in_specs=[smem, hbm, vmem, vmem],
            out_specs=[hbm, vmem],
            scratch_shapes=scratch,
            input_output_aliases={1: 0},
            compiler_params=params,
        )(half, field, after, factor_three)

    term, late = before
    nz, ny, length, _ = late.shape
    cut = k // (ny * nz)

    def body(half_ref, _, after_ref, factor_ref, term_ref, __, residual_ref, late_ref, field_ref, left_ref, sems, parted_ref):
        term, outs = compute(half_ref, after_ref, factor_ref, residual_ref, field_ref, left_ref, sems)
        parted = (term + term_ref[...]).T.reshape(ny, nz, cut, full_t)
        for z in range(nz):
            parted_ref[z] = parted[:, z]
        message = pltpu.make_async_copy(parted_ref, late_ref.at[:, :, pl.ds(length - cut, cut)], sems.at[2 * pieces])
        message.start()
        for copy in outs:
            copy.wait()
        message.wait()

    return pl.pallas_call(
        body,
        out_shape=[shape(rows, k), shape(*late.shape)],
        in_specs=[smem, hbm, vmem, vmem, vmem, hbm],
        out_specs=[hbm, hbm],
        scratch_shapes=scratch + [pltpu.VMEM((nz, ny, cut, full_t), f32)],
        input_output_aliases={1: 0, 5: 1},
        compiler_params=params,
    )(half, field, after, factor_three, term, late)


def mode_one_term(place, late, own_mine, own_other, near_mine, near_other, e):
    n, _, wide = late.shape
    q, t, r = own_mine.shape
    i = n * e
    group = min(q, 256 // t)

    def body(place_ref, late_ref, own_mine_ref, own_other_ref, near_mine_ref, near_other_ref, keep_ref, send_ref, rows_ref):
        rows_ref[...] = late_ref[:, pl.ds(0, e * q)].reshape(i * q, wide)
        first = place_ref[0] == 0
        sum_here = jnp.zeros((i, 2 * r), f32)
        for p in range(0, q, group):
            parts = [rows_ref[pl.ds(p + m, i, stride=q), :] for m in range(group)]
            low = jnp.concatenate([x[:, :t] for x in parts], axis=1)
            high = jnp.concatenate([x[:, t:] for x in parts], axis=1)
            for left, pair in (
                (jnp.where(first, low, high), (own_mine_ref, near_mine_ref)),
                (jnp.where(first, high, low), (own_other_ref, near_other_ref)),
            ):
                right = jnp.concatenate([ref[pl.ds(p, group)].reshape(group * t, r) for ref in pair], axis=1)
                sum_here = sum_here + product(left, right, ((1,), (0,)))
        same = place_ref[0] == place_ref[1]
        keep_ref[...] = jnp.where(same, sum_here[:, :r], sum_here[:, r:])
        send_ref[...] = jnp.where(same, sum_here[:, r:], sum_here[:, :r])

    return pl.pallas_call(
        body,
        out_shape=[shape(i, r), shape(i, r)],
        in_specs=[smem] + [vmem] * 5,
        out_specs=[vmem] * 2,
        scratch_shapes=[pltpu.VMEM((i * q, wide), f32)],
        compiler_params=params,
    )(place, late, own_mine, own_other, near_mine, near_other)


def local(tensor, core, factor_one, factor_two, factor_three):
    nx, ny, nz = lax.axis_size("gx"), lax.axis_size("gy"), lax.axis_size("gz")
    i, j, k = tensor.shape
    r, s, t = core.shape
    e, q, full_t, full_s, full_r = i // (ny * nz), s // nz, t * nz, s * ny, r * nx
    half_j, half_r, rows = j // nz, full_r // nz, i * j
    gx, gz = lax.axis_index("gx"), lax.axis_index("gz")
    place = jnp.stack([gz, gx]).astype(jnp.int32)
    flat = core.transpose(1, 2, 0)

    if nx == 2:
        other_one = swap(lax.dynamic_slice_in_dim(factor_one, (1 - gx) * r, r, axis=1), "gx")

    half = place[:1]
    field = tensor.reshape(rows, k)
    halves = tensor.reshape(nz, rows // nz, k)
    folded = swap(dot("ac,ct->at", part(halves, 1 - gz), factor_three), "gz")
    folded = folded + dot("ac,ct->at", part(halves, gz), factor_three)
    mine_two = part(factor_two.reshape(nz, half_j, full_s), gz)
    mine_two = jnp.concatenate([mine_two[:, c * full_t : (c + 1) * full_t] for c in range(full_s // full_t)], axis=0)
    early = jnp.concatenate(
        [folded.reshape(ny, e * j, full_t), jnp.broadcast_to(mine_two[None], (ny,) + mine_two.shape)], axis=1
    )
    if nx == 2:
        mine_one = lax.dynamic_slice_in_dim(factor_one, gx * r, r, axis=1)
        early, other_one = lax.optimization_barrier((early, other_one))
        sent = swap(mode_one(other_one, flat), "gx")
        after_one = mode_one(mine_one, flat) + sent
    else:
        every_one = trade(factor_one.reshape(i, nx, r).transpose(1, 0, 2), "gx")
        after_one = dot("xar,hqtr->xaqht", every_one, flat.reshape(nz, q, t, r)).reshape(nx, i, q, full_t)
        after_one = lax.psum_scatter(after_one, "gx", scatter_dimension=0)

    early = lax.all_to_all(early, "gy", 0, 0, tiled=True)
    early, after_one = lax.optimization_barrier((early, after_one))
    mine_two = early[:, e * j :].reshape(ny, full_s // full_t, half_j, full_t)
    other_two = swap(mine_two, "gz")
    gram = dot("ct,cu->tu", factor_three, factor_three)
    gram_other = swap(gram, "gz")

    flat = flat.reshape(nz, q, t, r)
    if nx == 2:
        own_mine, own_other = part(flat, gz), swap(part(flat, 1 - gz), "gz")
        near_mine = swap(own_mine, "gx")
    after_one = lax.all_to_all(after_one.reshape(nz * ny, e * q, full_t), ("gz", "gy"), 0, 0, tiled=True)
    after_one = after_one.reshape(nz, ny, e * q, full_t)
    one, two, moved = mode_two(place, after_one, mine_two, other_two, e, t)
    home = lax.all_to_all(moved, "gy", 0, 0, tiled=True).reshape(rows // nz, full_t)
    late, keep, send = back(place, moved, gram, gram_other, early, one, two, e * q + half_j + k // (ny * nz))
    late = put_two(late, keep, swap(send, "gz"), e * q)

    if nx == 2:
        home, late, near_mine = lax.optimization_barrier((home, late, near_mine))

    field, term_three = fit(half, field, home, factor_three)
    residual, late = fit(1 - half, field, swap(home, "gz"), factor_three, (term_three, late))
    late = lax.all_to_all(late.reshape((nz * ny,) + late.shape[2:]), ("gz", "gy"), 0, 0, tiled=True)
    sums = total(late[:, e * q :].reshape(nz, ny, -1, full_t).sum(axis=1), "gx")
    share_two, share_three = sums[:, :half_j], sums[:, half_j:]
    if nx == 2:
        keep_one, send_one = mode_one_term(place, late, own_mine, own_other, near_mine, swap(own_other, "gx"), e)
        term_one = keep_one + swap(send_one, "gz")
    else:
        share_one = late[:, : e * q].reshape(i, q, full_t)
        every_core = gather(trade(flat, "gz"), "gx")
        term_one = dot("aqht,xhqtr->axr", share_one.reshape(i, q, nz, t), every_core)
        term_one = lax.psum_scatter(term_one.reshape(i, nz, half_r).transpose(1, 0, 2), "gz", scatter_dimension=0)

    last = jnp.concatenate([term_one.reshape(-1, full_t), share_three.reshape(-1, full_t)], axis=0)
    last = lax.all_to_all(jnp.broadcast_to(last[None], (ny,) + last.shape), "gy", 0, 0, tiled=True)
    share_two = gather(share_two.reshape(j, full_s // nz), "gz")
    grad_two = jnp.concatenate([share_two[z] for z in range(nz)], axis=1) / jnp.sqrt(f32(i * nx * k * nz))
    last, grad_two = lax.optimization_barrier((last, grad_two))

    cut = i * half_r // full_t
    grad_one = gather(last[:, :cut].sum(axis=0).reshape(i, half_r), "gz")
    grad_one = jnp.concatenate([grad_one[z] for z in range(nz)], axis=1) / jnp.sqrt(f32(j * ny * k * nz))
    last = last[:, cut:].reshape(ny, nz, -1, full_t).transpose(1, 0, 2, 3)
    grad_three = trade(last, "gz").transpose(1, 0, 2, 3).reshape(k, full_t) / jnp.sqrt(f32(i * nx * j * ny))
    return (residual.reshape(i, j, k), grad_one, grad_two, grad_three)


def solution(mesh):
    placed = (P("gx", "gy", "gz"), P("gx", "gy", "gz"), P("gx", None), P("gy", None), P("gz", None))
    return jax.shard_map(
        local,
        mesh=mesh,
        in_specs=placed,
        out_specs=(P("gx", "gy", "gz"), P("gx", None), P("gy", None), P("gz", None)),
        check_vma=False,
    )
```

```python
import jax
import jax.numpy as jnp
from jax import lax
from jax.experimental import pallas as pl
from jax.experimental.pallas import tpu as pltpu
from jax.sharding import PartitionSpec as P

highest = lax.Precision.HIGHEST
f32 = jnp.float32
vmem = pl.BlockSpec(memory_space=pltpu.VMEM)
hbm = pl.BlockSpec(memory_space=pl.ANY)
smem = pl.BlockSpec(memory_space=pltpu.SMEM)
params = pltpu.CompilerParams(vmem_limit_bytes=14 * 1024 * 1024)


def shape(*sizes):
    return jax.ShapeDtypeStruct(sizes, f32)


def dot(spec, left, right):
    return jnp.einsum(spec, left, right, precision=highest)


def product(left, right, dims):
    return lax.dot_general(left, right, (dims, ((), ())), precision=highest, preferred_element_type=f32)


def swap(x, axis):
    return lax.ppermute(x, axis, [(0, 1), (1, 0)])


def part(x, index):
    return lax.dynamic_index_in_dim(x, index, 0, keepdims=False)


def in_order(axis, mine, other):
    first = lax.axis_index(axis) == 0
    return jnp.stack([jnp.where(first, mine, other), jnp.where(first, other, mine)])


def trade(x, axis):
    if lax.axis_size(axis) != 2:
        return lax.all_to_all(x, axis, 0, 0, tiled=True)
    me = lax.axis_index(axis)
    return in_order(axis, part(x, me), swap(part(x, 1 - me), axis))


def gather(x, axis):
    if lax.axis_size(axis) != 2:
        return lax.all_gather(x, axis)
    return in_order(axis, x, swap(x, axis))


def total(x, axis):
    if lax.axis_size(axis) != 2:
        return lax.psum(x, axis)
    return x + swap(x, axis)


def mode_one(rows, core):
    a, s, t = rows.shape[0], core.shape[0], core.shape[1]
    halves = 128 // t
    q = s // halves

    def body(rows_ref, core_ref, out_ref):
        right = jnp.concatenate([core_ref[h * q + n] for n in range(q) for h in range(halves)], axis=0)
        both = product(rows_ref[...], right, ((1,), (1,)))
        for n in range(q):
            out_ref[:, n, :] = both[:, n * halves * t : (n + 1) * halves * t]

    return pl.pallas_call(
        body,
        out_shape=shape(a, q, halves * t),
        in_specs=[vmem, vmem],
        out_specs=vmem,
        compiler_params=params,
        cost_estimate=pl.CostEstimate(flops=12 * a * s * t * 128, bytes_accessed=4 * s * t * 128, transcendentals=0),
    )(rows, core)


def mode_two(place, arrived, mine, other, e, t):
    nz, ny, rows, wide = arrived.shape
    q, halves, half_j, full_s = rows // e, wide // t, mine.shape[2], mine.shape[1] * wide
    j = nz * half_j

    def body(place_ref, arrived_ref, mine_ref, other_ref, one_ref, two_ref, moved_ref):
        me = place_ref[0]
        for c in range(mine_ref.shape[1]):
            here = pl.ds(c * wide, wide)
            two_ref[:, pl.ds(me, 1), :, here] = mine_ref[:, c][:, None]
            two_ref[:, pl.ds(1 - me, 1), :, here] = other_ref[:, c][:, None]
        for n in range(e):
            for h in range(halves):
                pieces = [arrived_ref[z, :, pl.ds(n * q, q), pl.ds(h * t, t)] for z in range(nz)]
                one_ref[:, h, :, pl.ds(n * wide, wide)] = jnp.concatenate(pieces, axis=-1)
        after = product(
            two_ref[...].reshape(ny * j, full_s), one_ref[...].reshape(full_s, e * wide), ((1,), (0,))
        )
        for n in range(e):
            moved_ref[:, n] = after[:, n * wide : (n + 1) * wide].reshape(ny, j, wide)

    one, two = (ny, halves, q, e * wide), (ny, nz, half_j, full_s)
    return pl.pallas_call(
        body,
        out_shape=[shape(*one), shape(*two), shape(ny, e, j, wide)],
        in_specs=[smem, vmem, vmem, vmem],
        out_specs=[vmem] * 3,
        compiler_params=params,
    )(place, arrived, mine, other)


def back(place, moved, gram, gram_other, early, one, two):
    ny, e, j, wide = moved.shape
    _, halves, q, _ = one.shape
    _, nz, half_j, full_s = two.shape
    edge, parts = e * q, full_s // wide

    def body(place_ref, moved_ref, gram_ref, gram_other_ref, early_ref, one_ref, two_ref, keep_ref, send_ref, sum_ref, wide_ref):
        me = place_ref[0]
        square = gram_ref[...] + gram_other_ref[...]
        whole_two = two_ref[...].reshape(ny * j, full_s)
        for n in range(e):
            folded = product(moved_ref[:, n].reshape(ny * j, wide), square, ((1,), (0,)))
            folded = folded - early_ref[:, pl.ds(n * j, j)].reshape(ny * j, wide)
            term = product(folded, one_ref[:, :, :, pl.ds(n * wide, wide)].reshape(full_s, wide), ((1,), (1,)))
            term = term.reshape(ny, nz, half_j, full_s)
            if n == 0:
                sum_ref[...] = term
            else:
                sum_ref[...] += term
            spread = product(whole_two, folded, ((0,), (0,))).reshape(ny, halves, q, wide)
            for h in range(halves):
                wide_ref[h, :, pl.ds(n * q, q)] = spread[:, h]
        for ref, z in ((keep_ref, me), (send_ref, 1 - me)):
            ref[:, pl.ds(0, edge)] = wide_ref[pl.ds(z, 1)].reshape(ny, edge, wide)
            for c in range(parts):
                piece = sum_ref[:, pl.ds(z, 1), :, pl.ds(c * wide, wide)]
                ref[:, pl.ds(edge + c * half_j, half_j)] = piece.reshape(ny, half_j, wide)

    return pl.pallas_call(
        body,
        out_shape=[shape(ny, edge + parts * half_j, wide)] * 2,
        in_specs=[smem] + [vmem] * 6,
        out_specs=[vmem] * 2,
        scratch_shapes=[pltpu.VMEM((ny, nz, half_j, full_s), f32), pltpu.VMEM((halves, ny, edge, wide), f32)],
        compiler_params=params,
        cost_estimate=pl.CostEstimate(flops=10**9, bytes_accessed=2**21, transcendentals=0),
    )(place, moved, gram, gram_other, early, one, two)


def put(keep, arrived, edge, length):
    ny, rows, wide = keep.shape

    def body(keep_ref, arrived_ref, late_ref, both_ref, sems):
        copies = [
            pltpu.make_async_copy(ref.at[:, pl.ds(0, edge)], late_ref.at[:, pl.ds(n * edge, edge)], sems.at[n])
            for n, ref in enumerate((keep_ref, arrived_ref))
        ]
        for copy in copies:
            copy.start()
        at = pl.ds(edge, rows - edge)
        both_ref[...] = keep_ref[:, at] + arrived_ref[:, at]
        last = pltpu.make_async_copy(both_ref, late_ref.at[:, pl.ds(2 * edge, rows - edge)], sems.at[2])
        last.start()
        for copy in copies + [last]:
            copy.wait()

    return pl.pallas_call(
        body,
        out_shape=shape(ny, length, wide),
        in_specs=[vmem, vmem],
        out_specs=hbm,
        scratch_shapes=[pltpu.VMEM((ny, rows - edge, wide), f32), pltpu.SemaphoreType.DMA((3,))],
        compiler_params=params,
    )(keep, arrived)


def fit(half, field, after, factor_three, before=None):
    rows, k = field.shape
    block, full_t = after.shape
    pieces = 1

    def compute(half_ref, after_ref, factor_ref, residual_ref, field_ref, left_ref, sems):
        cut = block // pieces
        ats = [pl.ds(pl.multiple_of(half_ref[0] * block + n * cut, cut), cut) for n in range(pieces)]
        here = [pl.ds(n * cut, cut) for n in range(pieces)]
        loads = [pltpu.make_async_copy(residual_ref.at[ats[n]], field_ref.at[here[n]], sems.at[n]) for n in range(pieces)]
        outs = [pltpu.make_async_copy(left_ref.at[here[n]], residual_ref.at[ats[n]], sems.at[pieces + n]) for n in range(pieces)]
        for copy in loads:
            copy.start()
        after = after_ref[...]
        left = product(after, factor_ref[...].T, ((1,), (0,)))
        for copy in loads:
            copy.wait()
        left = left - field_ref[...]
        left_ref[...] = left
        for copy in outs:
            copy.start()
        return product(after, left, ((0,), (0,))), outs

    scratch = [pltpu.VMEM((block, k), f32), pltpu.VMEM((block, k), f32), pltpu.SemaphoreType.DMA((2 * pieces + 1,))]
    if before is None:

        def body(half_ref, _, after_ref, factor_ref, residual_ref, term_ref, field_ref, left_ref, sems):
            term, outs = compute(half_ref, after_ref, factor_ref, residual_ref, field_ref, left_ref, sems)
            term_ref[...] = term
            for copy in outs:
                copy.wait()

        return pl.pallas_call(
            body,
            out_shape=[shape(rows, k), shape(full_t, k)],
            in_specs=[smem, hbm, vmem, vmem],
            out_specs=[hbm, vmem],
            scratch_shapes=scratch,
            input_output_aliases={1: 0},
            compiler_params=params,
        )(half, field, after, factor_three)

    term, late = before
    ny, length, _ = late.shape
    cut = k // ny

    def body(half_ref, _, after_ref, factor_ref, term_ref, __, residual_ref, late_ref, field_ref, left_ref, sems, parted_ref):
        term, outs = compute(half_ref, after_ref, factor_ref, residual_ref, field_ref, left_ref, sems)
        parted_ref[...] = (term + term_ref[...]).T.reshape(ny, cut, full_t)
        message = pltpu.make_async_copy(parted_ref, late_ref.at[:, pl.ds(length - cut, cut)], sems.at[2 * pieces])
        message.start()
        for copy in outs:
            copy.wait()
        message.wait()

    return pl.pallas_call(
        body,
        out_shape=[shape(rows, k), shape(*late.shape)],
        in_specs=[smem, hbm, vmem, vmem, vmem, hbm],
        out_specs=[hbm, hbm],
        scratch_shapes=scratch + [pltpu.VMEM((ny, cut, full_t), f32)],
        input_output_aliases={1: 0, 5: 1},
        compiler_params=params,
    )(half, field, after, factor_three, term, late)


def mode_one_term(place, late, own_mine, own_other, near_mine, near_other, e):
    ny, _, wide = late.shape
    q, t, r = own_mine.shape
    edge, half = e * q, ny * e * q
    i = 2 * ny * e
    group = min(q, 256 // t)

    def body(place_ref, late_ref, own_mine_ref, own_other_ref, near_mine_ref, near_other_ref, keep_ref, send_ref, rows_ref):
        for n, z in enumerate((place_ref[0], 1 - place_ref[0])):
            rows_ref[pl.ds(pl.multiple_of(z * half, half), half), :] = late_ref[:, pl.ds(n * edge, edge)].reshape(half, wide)
        first = place_ref[0] == 0
        sum_here = jnp.zeros((i, 2 * r), f32)
        for p in range(0, q, group):
            parts = [rows_ref[pl.ds(p + m, i, stride=q), :] for m in range(group)]
            low = jnp.concatenate([x[:, :t] for x in parts], axis=1)
            high = jnp.concatenate([x[:, t:] for x in parts], axis=1)
            for left, pair in (
                (jnp.where(first, low, high), (own_mine_ref, near_mine_ref)),
                (jnp.where(first, high, low), (own_other_ref, near_other_ref)),
            ):
                right = jnp.concatenate([ref[pl.ds(p, group)].reshape(group * t, r) for ref in pair], axis=1)
                sum_here = sum_here + product(left, right, ((1,), (0,)))
        same = place_ref[0] == place_ref[1]
        keep_ref[...] = jnp.where(same, sum_here[:, :r], sum_here[:, r:])
        send_ref[...] = jnp.where(same, sum_here[:, r:], sum_here[:, :r])

    return pl.pallas_call(
        body,
        out_shape=[shape(i, r), shape(i, r)],
        in_specs=[smem] + [vmem] * 5,
        out_specs=[vmem] * 2,
        scratch_shapes=[pltpu.VMEM((i * q, wide), f32)],
        compiler_params=params,
    )(place, late, own_mine, own_other, near_mine, near_other)


def local(tensor, core, factor_one, factor_two, factor_three):
    nx, ny, nz = lax.axis_size("gx"), lax.axis_size("gy"), lax.axis_size("gz")
    i, j, k = tensor.shape
    r, s, t = core.shape
    e, q, full_t, full_s, full_r = i // (ny * nz), s // nz, t * nz, s * ny, r * nx
    half_j, half_r, rows = j // nz, full_r // nz, i * j
    gx, gz = lax.axis_index("gx"), lax.axis_index("gz")
    place = jnp.stack([gz, gx]).astype(jnp.int32)
    flat = core.transpose(1, 2, 0)

    if nx == 2:
        other_one = swap(lax.dynamic_slice_in_dim(factor_one, (1 - gx) * r, r, axis=1), "gx")

    half = place[:1]
    field = tensor.reshape(rows, k)
    halves = tensor.reshape(nz, rows // nz, k)
    folded = swap(dot("ac,ct->at", part(halves, 1 - gz), factor_three), "gz")
    folded = folded + dot("ac,ct->at", part(halves, gz), factor_three)
    mine_two = part(factor_two.reshape(nz, half_j, full_s), gz)
    mine_two = jnp.concatenate([mine_two[:, c * full_t : (c + 1) * full_t] for c in range(full_s // full_t)], axis=0)
    early = jnp.concatenate(
        [folded.reshape(ny, e * j, full_t), jnp.broadcast_to(mine_two[None], (ny,) + mine_two.shape)], axis=1
    )
    if nx == 2:
        mine_one = lax.dynamic_slice_in_dim(factor_one, gx * r, r, axis=1)
        early, other_one = lax.optimization_barrier((early, other_one))
        sent = swap(mode_one(other_one, flat), "gx")
        after_one = mode_one(mine_one, flat) + sent
    else:
        every_one = trade(factor_one.reshape(i, nx, r).transpose(1, 0, 2), "gx")
        after_one = dot("xar,hqtr->xaqht", every_one, flat.reshape(nz, q, t, r)).reshape(nx, i, q, full_t)
        after_one = lax.psum_scatter(after_one, "gx", scatter_dimension=0)

    early = lax.all_to_all(early, "gy", 0, 0, tiled=True)
    early, after_one = lax.optimization_barrier((early, after_one))
    mine_two = early[:, e * j :].reshape(ny, full_s // full_t, half_j, full_t)
    other_two = swap(mine_two, "gz")
    gram = dot("ct,cu->tu", factor_three, factor_three)
    gram_other = swap(gram, "gz")

    flat = flat.reshape(nz, q, t, r)
    if nx == 2:
        own_mine, own_other = part(flat, gz), swap(part(flat, 1 - gz), "gz")
        near_mine = swap(own_mine, "gx")
    after_one = lax.all_to_all(after_one.reshape(nz * ny, e * q, full_t), ("gz", "gy"), 0, 0, tiled=True)
    after_one = after_one.reshape(nz, ny, e * q, full_t)
    one, two, moved = mode_two(place, after_one, mine_two, other_two, e, t)
    home = lax.all_to_all(moved, "gy", 0, 0, tiled=True).reshape(rows // nz, full_t)
    edge, parts = e * q, full_s // full_t
    keep, send = back(place, moved, gram, gram_other, early, one, two)
    late = put(keep, swap(send, "gz"), edge, 2 * edge + parts * half_j + k // ny)
    if nx == 2:
        home, late, near_mine = lax.optimization_barrier((home, late, near_mine))
    field, term_three = fit(half, field, home, factor_three)
    residual, late = fit(1 - half, field, swap(home, "gz"), factor_three, (term_three, late))
    late = lax.all_to_all(late, "gy", 0, 0, tiled=True)
    sums = total(late[:, 2 * edge :].sum(axis=0), "gx")
    share_two, share_three = sums[: parts * half_j], sums[parts * half_j :]
    if nx == 2:
        keep_one, send_one = mode_one_term(place, late, own_mine, own_other, near_mine, swap(own_other, "gx"), e)
        term_one = keep_one + swap(send_one, "gz")
    else:
        share_one = in_order("gz", late[:, :edge], late[:, edge : 2 * edge]).reshape(i, q, full_t)
        every_core = gather(trade(flat, "gz"), "gx")
        term_one = dot("aqht,xhqtr->axr", share_one.reshape(i, q, nz, t), every_core)
        term_one = lax.psum_scatter(term_one.reshape(i, nz, half_r).transpose(1, 0, 2), "gz", scatter_dimension=0)

    last = jnp.concatenate([term_one.reshape(-1, full_t), share_three], axis=0)
    last = lax.all_to_all(jnp.broadcast_to(last[None], (ny,) + last.shape), "gy", 0, 0, tiled=True)
    share_two = jnp.concatenate([share_two[c * half_j : (c + 1) * half_j] for c in range(parts)], axis=1)
    grad_two = gather(share_two, "gz").reshape(j, full_s) / jnp.sqrt(f32(i * nx * k * nz))
    last, grad_two = lax.optimization_barrier((last, grad_two))

    cut = i * half_r // full_t
    grad_one = gather(last[:, :cut].sum(axis=0).reshape(i, half_r), "gz")
    grad_one = jnp.concatenate([grad_one[z] for z in range(nz)], axis=1) / jnp.sqrt(f32(j * ny * k * nz))
    grad_three = last[:, cut:].reshape(k, full_t) / jnp.sqrt(f32(i * nx * j * ny))
    return (residual.reshape(i, j, k), grad_one, grad_two, grad_three)


def solution(mesh):
    placed = (P("gx", "gy", "gz"), P("gx", "gy", "gz"), P("gx", None), P("gy", None), P("gz", None))
    return jax.shard_map(
        local,
        mesh=mesh,
        in_specs=placed,
        out_specs=(P("gx", "gy", "gz"), P("gx", None), P("gy", None), P("gz", None)),
        check_vma=False,
    )
```

```python
import jax
import jax.numpy as jnp
from jax import lax
from jax.experimental import pallas as pl
from jax.experimental.pallas import tpu as pltpu
from jax.sharding import PartitionSpec as P

highest = lax.Precision.HIGHEST
f32 = jnp.float32
vmem = pl.BlockSpec(memory_space=pltpu.VMEM)
hbm = pl.BlockSpec(memory_space=pl.ANY)
smem = pl.BlockSpec(memory_space=pltpu.SMEM)
params = pltpu.CompilerParams(vmem_limit_bytes=14 * 1024 * 1024)


def shape(*sizes):
    return jax.ShapeDtypeStruct(sizes, f32)


def dot(spec, left, right):
    return jnp.einsum(spec, left, right, precision=highest)


def product(left, right, dims):
    return lax.dot_general(left, right, (dims, ((), ())), precision=highest, preferred_element_type=f32)


def swap(x, axis):
    return lax.ppermute(x, axis, [(0, 1), (1, 0)])


def part(x, index):
    return lax.dynamic_index_in_dim(x, index, 0, keepdims=False)


def in_order(axis, mine, other):
    first = lax.axis_index(axis) == 0
    return jnp.stack([jnp.where(first, mine, other), jnp.where(first, other, mine)])


def trade(x, axis):
    if lax.axis_size(axis) != 2:
        return lax.all_to_all(x, axis, 0, 0, tiled=True)
    me = lax.axis_index(axis)
    return in_order(axis, part(x, me), swap(part(x, 1 - me), axis))


def gather(x, axis):
    if lax.axis_size(axis) != 2:
        return lax.all_gather(x, axis)
    return in_order(axis, x, swap(x, axis))


def total(x, axis):
    if lax.axis_size(axis) != 2:
        return lax.psum(x, axis)
    return x + swap(x, axis)


def mode_one(rows, core):
    a, s, t = rows.shape[0], core.shape[0], core.shape[1]
    halves = 128 // t
    q = s // halves

    def body(rows_ref, core_ref, out_ref):
        right = jnp.concatenate([core_ref[h * q + n] for n in range(q) for h in range(halves)], axis=0)
        both = product(rows_ref[...], right, ((1,), (1,)))
        for n in range(q):
            out_ref[:, n, :] = both[:, n * halves * t : (n + 1) * halves * t]

    return pl.pallas_call(
        body,
        out_shape=shape(a, q, halves * t),
        in_specs=[vmem, vmem],
        out_specs=vmem,
        compiler_params=params,
        cost_estimate=pl.CostEstimate(flops=12 * a * s * t * 128, bytes_accessed=4 * s * t * 128, transcendentals=0),
    )(rows, core)


def mode_two(place, arrived, mine, other, e, t):
    nz, ny, rows, wide = arrived.shape
    q, halves, half_j, full_s = rows // e, wide // t, mine.shape[2], mine.shape[1] * wide
    j = nz * half_j

    def body(place_ref, arrived_ref, mine_ref, other_ref, one_ref, two_ref, moved_ref):
        me = place_ref[0]
        for c in range(mine_ref.shape[1]):
            here = pl.ds(c * wide, wide)
            two_ref[:, pl.ds(me, 1), :, here] = mine_ref[:, c][:, None]
            two_ref[:, pl.ds(1 - me, 1), :, here] = other_ref[:, c][:, None]
        for n in range(e):
            for h in range(halves):
                pieces = [arrived_ref[z, :, pl.ds(n * q, q), pl.ds(h * t, t)] for z in range(nz)]
                one_ref[:, h, :, pl.ds(n * wide, wide)] = jnp.concatenate(pieces, axis=-1)
        after = product(
            two_ref[...].reshape(ny * j, full_s), one_ref[...].reshape(full_s, e * wide), ((1,), (0,))
        )
        for n in range(e):
            moved_ref[:, n] = after[:, n * wide : (n + 1) * wide].reshape(ny, j, wide)

    one, two = (ny, halves, q, e * wide), (ny, nz, half_j, full_s)
    return pl.pallas_call(
        body,
        out_shape=[shape(*one), shape(*two), shape(ny, e, j, wide)],
        in_specs=[smem, vmem, vmem, vmem],
        out_specs=[vmem] * 3,
        compiler_params=params,
    )(place, arrived, mine, other)


def back(place, moved, gram, gram_other, early, one, two):
    ny, e, j, wide = moved.shape
    _, halves, q, _ = one.shape
    _, nz, half_j, full_s = two.shape
    edge, parts = e * q, full_s // wide

    def body(place_ref, moved_ref, gram_ref, gram_other_ref, early_ref, one_ref, two_ref, keep_ref, send_ref, sum_ref, wide_ref):
        me = place_ref[0]
        square = gram_ref[...] + gram_other_ref[...]
        whole_two = two_ref[...].reshape(ny * j, full_s)
        for n in range(e):
            folded = product(moved_ref[:, n].reshape(ny * j, wide), square, ((1,), (0,)))
            folded = folded - early_ref[:, pl.ds(n * j, j)].reshape(ny * j, wide)
            term = product(folded, one_ref[:, :, :, pl.ds(n * wide, wide)].reshape(full_s, wide), ((1,), (1,)))
            term = term.reshape(ny, nz, half_j, full_s)
            if n == 0:
                sum_ref[...] = term
            else:
                sum_ref[...] += term
            spread = product(whole_two, folded, ((0,), (0,))).reshape(ny, halves, q, wide)
            for h in range(halves):
                wide_ref[h, :, pl.ds(n * q, q)] = spread[:, h]
        for ref, z in ((keep_ref, me), (send_ref, 1 - me)):
            ref[:, pl.ds(0, edge)] = wide_ref[pl.ds(z, 1)].reshape(ny, edge, wide)
            for c in range(parts):
                piece = sum_ref[:, pl.ds(z, 1), :, pl.ds(c * wide, wide)]
                ref[:, pl.ds(edge + c * half_j, half_j)] = piece.reshape(ny, half_j, wide)

    return pl.pallas_call(
        body,
        out_shape=[shape(ny, edge + parts * half_j, wide)] * 2,
        in_specs=[smem] + [vmem] * 6,
        out_specs=[vmem] * 2,
        scratch_shapes=[pltpu.VMEM((ny, nz, half_j, full_s), f32), pltpu.VMEM((halves, ny, edge, wide), f32)],
        compiler_params=params,
        cost_estimate=pl.CostEstimate(flops=10**9, bytes_accessed=2**21, transcendentals=0),
    )(place, moved, gram, gram_other, early, one, two)


def put(keep, arrived, edge, length):
    ny, rows, wide = keep.shape

    def body(keep_ref, arrived_ref, late_ref, both_ref, sems):
        copies = [
            pltpu.make_async_copy(ref.at[:, pl.ds(0, edge)], late_ref.at[:, pl.ds(n * edge, edge)], sems.at[n])
            for n, ref in enumerate((keep_ref, arrived_ref))
        ]
        for copy in copies:
            copy.start()
        at = pl.ds(edge, rows - edge)
        both_ref[...] = keep_ref[:, at] + arrived_ref[:, at]
        last = pltpu.make_async_copy(both_ref, late_ref.at[:, pl.ds(2 * edge, rows - edge)], sems.at[2])
        last.start()
        for copy in copies + [last]:
            copy.wait()

    return pl.pallas_call(
        body,
        out_shape=shape(ny, length, wide),
        in_specs=[vmem, vmem],
        out_specs=hbm,
        scratch_shapes=[pltpu.VMEM((ny, rows - edge, wide), f32), pltpu.SemaphoreType.DMA((3,))],
        compiler_params=params,
    )(keep, arrived)


def fit(half, field, after, factor_three, before=None):
    rows, k = field.shape
    block, full_t = after.shape
    pieces = 1

    def compute(half_ref, after_ref, factor_ref, residual_ref, field_ref, left_ref, sems):
        cut = block // pieces
        ats = [pl.ds(pl.multiple_of(half_ref[0] * block + n * cut, cut), cut) for n in range(pieces)]
        here = [pl.ds(n * cut, cut) for n in range(pieces)]
        loads = [pltpu.make_async_copy(residual_ref.at[ats[n]], field_ref.at[here[n]], sems.at[n]) for n in range(pieces)]
        outs = [pltpu.make_async_copy(left_ref.at[here[n]], residual_ref.at[ats[n]], sems.at[pieces + n]) for n in range(pieces)]
        for copy in loads:
            copy.start()
        after = after_ref[...]
        left = product(after, factor_ref[...].T, ((1,), (0,)))
        for copy in loads:
            copy.wait()
        left = left - field_ref[...]
        left_ref[...] = left
        for copy in outs:
            copy.start()
        return product(after, left, ((0,), (0,))), outs

    scratch = [pltpu.VMEM((block, k), f32), pltpu.VMEM((block, k), f32), pltpu.SemaphoreType.DMA((2 * pieces + 1,))]
    if before is None:

        def body(half_ref, _, after_ref, factor_ref, residual_ref, term_ref, field_ref, left_ref, sems):
            term, outs = compute(half_ref, after_ref, factor_ref, residual_ref, field_ref, left_ref, sems)
            term_ref[...] = term
            for copy in outs:
                copy.wait()

        return pl.pallas_call(
            body,
            out_shape=[shape(rows, k), shape(full_t, k)],
            in_specs=[smem, hbm, vmem, vmem],
            out_specs=[hbm, vmem],
            scratch_shapes=scratch,
            input_output_aliases={1: 0},
            compiler_params=params,
        )(half, field, after, factor_three)

    term, late = before
    ny, length, _ = late.shape
    cut = k // ny

    def body(half_ref, _, after_ref, factor_ref, term_ref, __, residual_ref, late_ref, field_ref, left_ref, sems, parted_ref):
        term, outs = compute(half_ref, after_ref, factor_ref, residual_ref, field_ref, left_ref, sems)
        parted_ref[...] = (term + term_ref[...]).T.reshape(ny, cut, full_t)
        message = pltpu.make_async_copy(parted_ref, late_ref.at[:, pl.ds(length - cut, cut)], sems.at[2 * pieces])
        message.start()
        for copy in outs:
            copy.wait()
        message.wait()

    return pl.pallas_call(
        body,
        out_shape=[shape(rows, k), shape(*late.shape)],
        in_specs=[smem, hbm, vmem, vmem, vmem, hbm],
        out_specs=[hbm, hbm],
        scratch_shapes=scratch + [pltpu.VMEM((ny, cut, full_t), f32)],
        input_output_aliases={1: 0, 5: 1},
        compiler_params=params,
    )(half, field, after, factor_three, term, late)


def mode_one_term(place, late, own_mine, own_other, near_mine, near_other, e):
    ny, _, wide = late.shape
    q, t, r = own_mine.shape
    edge, half = e * q, ny * e * q
    i = 2 * ny * e
    group = min(q, 256 // t)

    def body(place_ref, late_ref, own_mine_ref, own_other_ref, near_mine_ref, near_other_ref, keep_ref, send_ref, rows_ref):
        for n, z in enumerate((place_ref[0], 1 - place_ref[0])):
            rows_ref[pl.ds(pl.multiple_of(z * half, half), half), :] = late_ref[:, pl.ds(n * edge, edge)].reshape(half, wide)
        first = place_ref[0] == 0
        sum_here = jnp.zeros((i, 2 * r), f32)
        for p in range(0, q, group):
            parts = [rows_ref[pl.ds(p + m, i, stride=q), :] for m in range(group)]
            low = jnp.concatenate([x[:, :t] for x in parts], axis=1)
            high = jnp.concatenate([x[:, t:] for x in parts], axis=1)
            for left, pair in (
                (jnp.where(first, low, high), (own_mine_ref, near_mine_ref)),
                (jnp.where(first, high, low), (own_other_ref, near_other_ref)),
            ):
                right = jnp.concatenate([ref[pl.ds(p, group)].reshape(group * t, r) for ref in pair], axis=1)
                sum_here = sum_here + product(left, right, ((1,), (0,)))
        same = place_ref[0] == place_ref[1]
        keep_ref[...] = jnp.where(same, sum_here[:, :r], sum_here[:, r:])
        send_ref[...] = jnp.where(same, sum_here[:, r:], sum_here[:, :r])

    return pl.pallas_call(
        body,
        out_shape=[shape(i, r), shape(i, r)],
        in_specs=[smem] + [vmem] * 5,
        out_specs=[vmem] * 2,
        scratch_shapes=[pltpu.VMEM((i * q, wide), f32)],
        compiler_params=params,
    )(place, late, own_mine, own_other, near_mine, near_other)


def local(tensor, core, factor_one, factor_two, factor_three):
    nx, ny, nz = lax.axis_size("gx"), lax.axis_size("gy"), lax.axis_size("gz")
    i, j, k = tensor.shape
    r, s, t = core.shape
    e, q, full_t, full_s, full_r = i // (ny * nz), s // nz, t * nz, s * ny, r * nx
    half_j, half_r, rows = j // nz, full_r // nz, i * j
    gx, gz = lax.axis_index("gx"), lax.axis_index("gz")
    place = jnp.stack([gz, gx]).astype(jnp.int32)
    flat = core.transpose(1, 2, 0)

    if nx == 2:
        other_one = swap(lax.dynamic_slice_in_dim(factor_one, (1 - gx) * r, r, axis=1), "gx")

    half = place[:1]
    field = tensor.reshape(rows, k)
    halves = tensor.reshape(nz, rows // nz, k)
    folded = swap(dot("ac,ct->at", part(halves, 1 - gz), factor_three), "gz")
    folded = folded + dot("ac,ct->at", part(halves, gz), factor_three)
    mine_two = part(factor_two.reshape(nz, half_j, full_s), gz)
    mine_two = jnp.concatenate([mine_two[:, c * full_t : (c + 1) * full_t] for c in range(full_s // full_t)], axis=0)
    early = jnp.concatenate(
        [folded.reshape(ny, e * j, full_t), jnp.broadcast_to(mine_two[None], (ny,) + mine_two.shape)], axis=1
    )
    if nx == 2:
        mine_one = lax.dynamic_slice_in_dim(factor_one, gx * r, r, axis=1)
        early, other_one = lax.optimization_barrier((early, other_one))
        sent = swap(mode_one(other_one, flat), "gx")
        after_one = mode_one(mine_one, flat) + sent
    else:
        every_one = trade(factor_one.reshape(i, nx, r).transpose(1, 0, 2), "gx")
        after_one = dot("xar,hqtr->xaqht", every_one, flat.reshape(nz, q, t, r)).reshape(nx, i, q, full_t)
        after_one = lax.psum_scatter(after_one, "gx", scatter_dimension=0)

    early = lax.all_to_all(early, "gy", 0, 0, tiled=True)
    early, after_one = lax.optimization_barrier((early, after_one))
    mine_two = early[:, e * j :].reshape(ny, full_s // full_t, half_j, full_t)
    other_two = swap(mine_two, "gz")
    gram = dot("ct,cu->tu", factor_three, factor_three)
    gram_other = swap(gram, "gz")

    flat = flat.reshape(nz, q, t, r)
    if nx == 2:
        own_mine, own_other = part(flat, gz), swap(part(flat, 1 - gz), "gz")
        near_mine = swap(own_mine, "gx")
    after_one = lax.all_to_all(after_one.reshape(nz * ny, e * q, full_t), ("gz", "gy"), 0, 0, tiled=True)
    after_one, gram_other = lax.optimization_barrier((after_one, gram_other))
    after_one = after_one.reshape(nz, ny, e * q, full_t)
    one, two, moved = mode_two(place, after_one, mine_two, other_two, e, t)
    home = lax.all_to_all(moved, "gy", 0, 0, tiled=True).reshape(rows // nz, full_t)
    edge, parts = e * q, full_s // full_t
    keep, send = back(place, moved, gram, gram_other, early, one, two)
    late = put(keep, swap(send, "gz"), edge, 2 * edge + parts * half_j + k // ny)
    if nx == 2:
        home, late, near_mine = lax.optimization_barrier((home, late, near_mine))
    field, term_three = fit(half, field, home, factor_three)
    residual, late = fit(1 - half, field, swap(home, "gz"), factor_three, (term_three, late))
    late = lax.all_to_all(late, "gy", 0, 0, tiled=True)
    sums = total(late[:, 2 * edge :].sum(axis=0), "gx")
    share_two, share_three = sums[: parts * half_j], sums[parts * half_j :]
    if nx == 2:
        keep_one, send_one = mode_one_term(place, late, own_mine, own_other, near_mine, swap(own_other, "gx"), e)
        term_one = keep_one + swap(send_one, "gz")
    else:
        share_one = in_order("gz", late[:, :edge], late[:, edge : 2 * edge]).reshape(i, q, full_t)
        every_core = gather(trade(flat, "gz"), "gx")
        term_one = dot("aqht,xhqtr->axr", share_one.reshape(i, q, nz, t), every_core)
        term_one = lax.psum_scatter(term_one.reshape(i, nz, half_r).transpose(1, 0, 2), "gz", scatter_dimension=0)

    last = jnp.concatenate([term_one.reshape(-1, full_t), share_three], axis=0)
    last = lax.all_to_all(jnp.broadcast_to(last[None], (ny,) + last.shape), "gy", 0, 0, tiled=True)
    share_two = jnp.concatenate([share_two[c * half_j : (c + 1) * half_j] for c in range(parts)], axis=1)
    grad_two = gather(share_two, "gz").reshape(j, full_s) / jnp.sqrt(f32(i * nx * k * nz))
    last, grad_two = lax.optimization_barrier((last, grad_two))

    cut = i * half_r // full_t
    grad_one = gather(last[:, :cut].sum(axis=0).reshape(i, half_r), "gz")
    grad_one = jnp.concatenate([grad_one[z] for z in range(nz)], axis=1) / jnp.sqrt(f32(j * ny * k * nz))
    grad_three = last[:, cut:].reshape(k, full_t) / jnp.sqrt(f32(i * nx * j * ny))
    return (residual.reshape(i, j, k), grad_one, grad_two, grad_three)


def solution(mesh):
    placed = (P("gx", "gy", "gz"), P("gx", "gy", "gz"), P("gx", None), P("gy", None), P("gz", None))
    return jax.shard_map(
        local,
        mesh=mesh,
        in_specs=placed,
        out_specs=(P("gx", "gy", "gz"), P("gx", None), P("gy", None), P("gz", None)),
        check_vma=False,
    )
```

```python
import jax
import jax.numpy as jnp
from jax import lax
from jax.experimental import pallas as pl
from jax.experimental.pallas import tpu as pltpu
from jax.sharding import PartitionSpec as P

highest = lax.Precision.HIGHEST
f32 = jnp.float32
vmem = pl.BlockSpec(memory_space=pltpu.VMEM)
hbm = pl.BlockSpec(memory_space=pl.ANY)
smem = pl.BlockSpec(memory_space=pltpu.SMEM)
params = pltpu.CompilerParams(vmem_limit_bytes=14 * 1024 * 1024)


def shape(*sizes):
    return jax.ShapeDtypeStruct(sizes, f32)


def dot(spec, left, right):
    return jnp.einsum(spec, left, right, precision=highest)


def product(left, right, dims):
    return lax.dot_general(left, right, (dims, ((), ())), precision=highest, preferred_element_type=f32)


def swap(x, axis):
    return lax.ppermute(x, axis, [(0, 1), (1, 0)])


def part(x, index):
    return lax.dynamic_index_in_dim(x, index, 0, keepdims=False)


def in_order(axis, mine, other):
    first = lax.axis_index(axis) == 0
    return jnp.stack([jnp.where(first, mine, other), jnp.where(first, other, mine)])


def trade(x, axis):
    if lax.axis_size(axis) != 2:
        return lax.all_to_all(x, axis, 0, 0, tiled=True)
    me = lax.axis_index(axis)
    return in_order(axis, part(x, me), swap(part(x, 1 - me), axis))


def gather(x, axis):
    if lax.axis_size(axis) != 2:
        return lax.all_gather(x, axis)
    return in_order(axis, x, swap(x, axis))


def total(x, axis):
    if lax.axis_size(axis) != 2:
        return lax.psum(x, axis)
    return x + swap(x, axis)


def mode_one(rows, core):
    a, s, t = rows.shape[0], core.shape[0], core.shape[1]
    halves = 128 // t
    q = s // halves

    def body(rows_ref, core_ref, out_ref):
        right = jnp.concatenate([core_ref[h * q + n] for n in range(q) for h in range(halves)], axis=0)
        both = product(rows_ref[...], right, ((1,), (1,)))
        for n in range(q):
            out_ref[:, n, :] = both[:, n * halves * t : (n + 1) * halves * t]

    return pl.pallas_call(
        body,
        out_shape=shape(a, q, halves * t),
        in_specs=[vmem, vmem],
        out_specs=vmem,
        compiler_params=params,
        cost_estimate=pl.CostEstimate(flops=12 * a * s * t * 128, bytes_accessed=4 * s * t * 128, transcendentals=0),
    )(rows, core)


def order_two(place, mine, other):
    ny, parts, half_j, wide = mine.shape

    def body(place_ref, mine_ref, other_ref, two_ref):
        me = place_ref[0]
        for c in range(parts):
            here = pl.ds(c * wide, wide)
            two_ref[:, pl.ds(me, 1), :, here] = mine_ref[:, c][:, None]
            two_ref[:, pl.ds(1 - me, 1), :, here] = other_ref[:, c][:, None]

    return pl.pallas_call(
        body,
        out_shape=shape(ny, 2, half_j, parts * wide),
        in_specs=[smem, vmem, vmem],
        out_specs=vmem,
        compiler_params=params,
    )(place, mine, other)


def mode_two(arrived, two, e, t):
    nz, ny, rows, wide = arrived.shape
    q, halves, half_j, full_s = rows // e, wide // t, two.shape[2], two.shape[3]
    j = nz * half_j

    def body(arrived_ref, two_ref, one_ref, moved_ref):
        for n in range(e):
            for h in range(halves):
                pieces = [arrived_ref[z, :, pl.ds(n * q, q), pl.ds(h * t, t)] for z in range(nz)]
                one_ref[:, h, :, pl.ds(n * wide, wide)] = jnp.concatenate(pieces, axis=-1)
        after = product(
            two_ref[...].reshape(ny * j, full_s), one_ref[...].reshape(full_s, e * wide), ((1,), (0,))
        )
        for n in range(e):
            moved_ref[:, n] = after[:, n * wide : (n + 1) * wide].reshape(ny, j, wide)

    return pl.pallas_call(
        body,
        out_shape=[shape(ny, halves, q, e * wide), shape(ny, e, j, wide)],
        in_specs=[vmem, vmem],
        out_specs=[vmem] * 2,
        compiler_params=params,
    )(arrived, two)


def back(place, moved, gram, gram_other, early, one, two):
    ny, e, j, wide = moved.shape
    _, halves, q, _ = one.shape
    _, nz, half_j, full_s = two.shape
    edge, parts = e * q, full_s // wide

    def body(place_ref, moved_ref, gram_ref, gram_other_ref, early_ref, one_ref, two_ref, keep_ref, send_ref, sum_ref, wide_ref):
        me = place_ref[0]
        square = gram_ref[...] + gram_other_ref[...]
        whole_two = two_ref[...].reshape(ny * j, full_s)
        for n in range(e):
            folded = product(moved_ref[:, n].reshape(ny * j, wide), square, ((1,), (0,)))
            folded = folded - early_ref[:, pl.ds(n * j, j)].reshape(ny * j, wide)
            term = product(folded, one_ref[:, :, :, pl.ds(n * wide, wide)].reshape(full_s, wide), ((1,), (1,)))
            term = term.reshape(ny, nz, half_j, full_s)
            if n == 0:
                sum_ref[...] = term
            else:
                sum_ref[...] += term
            spread = product(whole_two, folded, ((0,), (0,))).reshape(ny, halves, q, wide)
            for h in range(halves):
                wide_ref[h, :, pl.ds(n * q, q)] = spread[:, h]
        for ref, z in ((keep_ref, me), (send_ref, 1 - me)):
            ref[:, pl.ds(0, edge)] = wide_ref[pl.ds(z, 1)].reshape(ny, edge, wide)
            for c in range(parts):
                piece = sum_ref[:, pl.ds(z, 1), :, pl.ds(c * wide, wide)]
                ref[:, pl.ds(edge + c * half_j, half_j)] = piece.reshape(ny, half_j, wide)

    return pl.pallas_call(
        body,
        out_shape=[shape(ny, edge + parts * half_j, wide)] * 2,
        in_specs=[smem] + [vmem] * 6,
        out_specs=[vmem] * 2,
        scratch_shapes=[pltpu.VMEM((ny, nz, half_j, full_s), f32), pltpu.VMEM((halves, ny, edge, wide), f32)],
        compiler_params=params,
        cost_estimate=pl.CostEstimate(flops=10**9, bytes_accessed=2**21, transcendentals=0),
    )(place, moved, gram, gram_other, early, one, two)


def put(keep, arrived, edge, length):
    ny, rows, wide = keep.shape

    def body(keep_ref, arrived_ref, late_ref, both_ref, sems):
        copies = [
            pltpu.make_async_copy(ref.at[:, pl.ds(0, edge)], late_ref.at[:, pl.ds(n * edge, edge)], sems.at[n])
            for n, ref in enumerate((keep_ref, arrived_ref))
        ]
        for copy in copies:
            copy.start()
        at = pl.ds(edge, rows - edge)
        both_ref[...] = keep_ref[:, at] + arrived_ref[:, at]
        last = pltpu.make_async_copy(both_ref, late_ref.at[:, pl.ds(2 * edge, rows - edge)], sems.at[2])
        last.start()
        for copy in copies + [last]:
            copy.wait()

    return pl.pallas_call(
        body,
        out_shape=shape(ny, length, wide),
        in_specs=[vmem, vmem],
        out_specs=hbm,
        scratch_shapes=[pltpu.VMEM((ny, rows - edge, wide), f32), pltpu.SemaphoreType.DMA((3,))],
        compiler_params=params,
    )(keep, arrived)


def fit(half, field, after, factor_three, before=None):
    rows, k = field.shape
    block, full_t = after.shape
    pieces = 1

    def compute(half_ref, after_ref, factor_ref, residual_ref, field_ref, left_ref, sems):
        cut = block // pieces
        ats = [pl.ds(pl.multiple_of(half_ref[0] * block + n * cut, cut), cut) for n in range(pieces)]
        here = [pl.ds(n * cut, cut) for n in range(pieces)]
        loads = [pltpu.make_async_copy(residual_ref.at[ats[n]], field_ref.at[here[n]], sems.at[n]) for n in range(pieces)]
        outs = [pltpu.make_async_copy(left_ref.at[here[n]], residual_ref.at[ats[n]], sems.at[pieces + n]) for n in range(pieces)]
        for copy in loads:
            copy.start()
        after = after_ref[...]
        left = product(after, factor_ref[...].T, ((1,), (0,)))
        for copy in loads:
            copy.wait()
        left = left - field_ref[...]
        left_ref[...] = left
        for copy in outs:
            copy.start()
        return product(after, left, ((0,), (0,))), outs

    scratch = [pltpu.VMEM((block, k), f32), pltpu.VMEM((block, k), f32), pltpu.SemaphoreType.DMA((2 * pieces + 1,))]
    if before is None:

        def body(half_ref, _, after_ref, factor_ref, residual_ref, term_ref, field_ref, left_ref, sems):
            term, outs = compute(half_ref, after_ref, factor_ref, residual_ref, field_ref, left_ref, sems)
            term_ref[...] = term
            for copy in outs:
                copy.wait()

        return pl.pallas_call(
            body,
            out_shape=[shape(rows, k), shape(full_t, k)],
            in_specs=[smem, hbm, vmem, vmem],
            out_specs=[hbm, vmem],
            scratch_shapes=scratch,
            input_output_aliases={1: 0},
            compiler_params=params,
        )(half, field, after, factor_three)

    term, late = before
    ny, length, _ = late.shape
    cut = k // ny

    def body(half_ref, _, after_ref, factor_ref, term_ref, __, residual_ref, late_ref, field_ref, left_ref, sems, parted_ref):
        term, outs = compute(half_ref, after_ref, factor_ref, residual_ref, field_ref, left_ref, sems)
        parted_ref[...] = (term + term_ref[...]).T.reshape(ny, cut, full_t)
        message = pltpu.make_async_copy(parted_ref, late_ref.at[:, pl.ds(length - cut, cut)], sems.at[2 * pieces])
        message.start()
        for copy in outs:
            copy.wait()
        message.wait()

    return pl.pallas_call(
        body,
        out_shape=[shape(rows, k), shape(*late.shape)],
        in_specs=[smem, hbm, vmem, vmem, vmem, hbm],
        out_specs=[hbm, hbm],
        scratch_shapes=scratch + [pltpu.VMEM((ny, cut, full_t), f32)],
        input_output_aliases={1: 0, 5: 1},
        compiler_params=params,
    )(half, field, after, factor_three, term, late)


def mode_one_term(place, late, own_mine, own_other, near_mine, near_other, e):
    ny, _, wide = late.shape
    q, t, r = own_mine.shape
    edge, half = e * q, ny * e * q
    i = 2 * ny * e
    group = min(q, 256 // t)

    def body(place_ref, late_ref, own_mine_ref, own_other_ref, near_mine_ref, near_other_ref, keep_ref, send_ref, rows_ref):
        for n, z in enumerate((place_ref[0], 1 - place_ref[0])):
            rows_ref[pl.ds(pl.multiple_of(z * half, half), half), :] = late_ref[:, pl.ds(n * edge, edge)].reshape(half, wide)
        first = place_ref[0] == 0
        sum_here = jnp.zeros((i, 2 * r), f32)
        for p in range(0, q, group):
            parts = [rows_ref[pl.ds(p + m, i, stride=q), :] for m in range(group)]
            low = jnp.concatenate([x[:, :t] for x in parts], axis=1)
            high = jnp.concatenate([x[:, t:] for x in parts], axis=1)
            for left, pair in (
                (jnp.where(first, low, high), (own_mine_ref, near_mine_ref)),
                (jnp.where(first, high, low), (own_other_ref, near_other_ref)),
            ):
                right = jnp.concatenate([ref[pl.ds(p, group)].reshape(group * t, r) for ref in pair], axis=1)
                sum_here = sum_here + product(left, right, ((1,), (0,)))
        same = place_ref[0] == place_ref[1]
        keep_ref[...] = jnp.where(same, sum_here[:, :r], sum_here[:, r:])
        send_ref[...] = jnp.where(same, sum_here[:, r:], sum_here[:, :r])

    return pl.pallas_call(
        body,
        out_shape=[shape(i, r), shape(i, r)],
        in_specs=[smem] + [vmem] * 5,
        out_specs=[vmem] * 2,
        scratch_shapes=[pltpu.VMEM((i * q, wide), f32)],
        compiler_params=params,
    )(place, late, own_mine, own_other, near_mine, near_other)


def local(tensor, core, factor_one, factor_two, factor_three):
    nx, ny, nz = lax.axis_size("gx"), lax.axis_size("gy"), lax.axis_size("gz")
    i, j, k = tensor.shape
    r, s, t = core.shape
    e, q, full_t, full_s, full_r = i // (ny * nz), s // nz, t * nz, s * ny, r * nx
    half_j, half_r, rows = j // nz, full_r // nz, i * j
    gx, gz = lax.axis_index("gx"), lax.axis_index("gz")
    place = jnp.stack([gz, gx]).astype(jnp.int32)
    flat = core.transpose(1, 2, 0)

    if nx == 2:
        other_one = swap(lax.dynamic_slice_in_dim(factor_one, (1 - gx) * r, r, axis=1), "gx")

    half = place[:1]
    field = tensor.reshape(rows, k)
    halves = tensor.reshape(nz, rows // nz, k)
    folded = swap(dot("ac,ct->at", part(halves, 1 - gz), factor_three), "gz")
    folded = folded + dot("ac,ct->at", part(halves, gz), factor_three)
    mine_two = part(factor_two.reshape(nz, half_j, full_s), gz)
    mine_two = jnp.concatenate([mine_two[:, c * full_t : (c + 1) * full_t] for c in range(full_s // full_t)], axis=0)
    early = jnp.concatenate(
        [folded.reshape(ny, e * j, full_t), jnp.broadcast_to(mine_two[None], (ny,) + mine_two.shape)], axis=1
    )
    if nx == 2:
        mine_one = lax.dynamic_slice_in_dim(factor_one, gx * r, r, axis=1)
        early, other_one = lax.optimization_barrier((early, other_one))
        sent = swap(mode_one(other_one, flat), "gx")
        after_one = mode_one(mine_one, flat) + sent
    else:
        every_one = trade(factor_one.reshape(i, nx, r).transpose(1, 0, 2), "gx")
        after_one = dot("xar,hqtr->xaqht", every_one, flat.reshape(nz, q, t, r)).reshape(nx, i, q, full_t)
        after_one = lax.psum_scatter(after_one, "gx", scatter_dimension=0)

    early = lax.all_to_all(early, "gy", 0, 0, tiled=True)
    early, after_one = lax.optimization_barrier((early, after_one))
    mine_two = early[:, e * j :].reshape(ny, full_s // full_t, half_j, full_t)
    other_two = swap(mine_two, "gz")
    gram = dot("ct,cu->tu", factor_three, factor_three)
    gram_other = swap(gram, "gz")

    flat = flat.reshape(nz, q, t, r)
    if nx == 2:
        own_mine, own_other = part(flat, gz), swap(part(flat, 1 - gz), "gz")
        near_mine = swap(own_mine, "gx")
    after_one = lax.all_to_all(after_one.reshape(nz * ny, e * q, full_t), ("gz", "gy"), 0, 0, tiled=True)
    two = order_two(place, mine_two, other_two)
    after_one, gram_other, two = lax.optimization_barrier((after_one, gram_other, two))
    after_one = after_one.reshape(nz, ny, e * q, full_t)
    one, moved = mode_two(after_one, two, e, t)
    home = lax.all_to_all(moved, "gy", 0, 0, tiled=True).reshape(rows // nz, full_t)
    edge, parts = e * q, full_s // full_t
    keep, send = back(place, moved, gram, gram_other, early, one, two)
    late = put(keep, swap(send, "gz"), edge, 2 * edge + parts * half_j + k // ny)
    if nx == 2:
        home, late, near_mine = lax.optimization_barrier((home, late, near_mine))
    field, term_three = fit(half, field, home, factor_three)
    residual, late = fit(1 - half, field, swap(home, "gz"), factor_three, (term_three, late))
    late = lax.all_to_all(late, "gy", 0, 0, tiled=True)
    sums = total(late[:, 2 * edge :].sum(axis=0), "gx")
    share_two, share_three = sums[: parts * half_j], sums[parts * half_j :]
    if nx == 2:
        keep_one, send_one = mode_one_term(place, late, own_mine, own_other, near_mine, swap(own_other, "gx"), e)
        term_one = keep_one + swap(send_one, "gz")
    else:
        share_one = in_order("gz", late[:, :edge], late[:, edge : 2 * edge]).reshape(i, q, full_t)
        every_core = gather(trade(flat, "gz"), "gx")
        term_one = dot("aqht,xhqtr->axr", share_one.reshape(i, q, nz, t), every_core)
        term_one = lax.psum_scatter(term_one.reshape(i, nz, half_r).transpose(1, 0, 2), "gz", scatter_dimension=0)

    last = jnp.concatenate([term_one.reshape(-1, full_t), share_three], axis=0)
    last = lax.all_to_all(jnp.broadcast_to(last[None], (ny,) + last.shape), "gy", 0, 0, tiled=True)
    share_two = jnp.concatenate([share_two[c * half_j : (c + 1) * half_j] for c in range(parts)], axis=1)
    grad_two = gather(share_two, "gz").reshape(j, full_s) / jnp.sqrt(f32(i * nx * k * nz))
    last, grad_two = lax.optimization_barrier((last, grad_two))

    cut = i * half_r // full_t
    grad_one = gather(last[:, :cut].sum(axis=0).reshape(i, half_r), "gz")
    grad_one = jnp.concatenate([grad_one[z] for z in range(nz)], axis=1) / jnp.sqrt(f32(j * ny * k * nz))
    grad_three = last[:, cut:].reshape(k, full_t) / jnp.sqrt(f32(i * nx * j * ny))
    return (residual.reshape(i, j, k), grad_one, grad_two, grad_three)


def solution(mesh):
    placed = (P("gx", "gy", "gz"), P("gx", "gy", "gz"), P("gx", None), P("gy", None), P("gz", None))
    return jax.shard_map(
        local,
        mesh=mesh,
        in_specs=placed,
        out_specs=(P("gx", "gy", "gz"), P("gx", None), P("gy", None), P("gz", None)),
        check_vma=False,
    )
```

```python
import jax
import jax.numpy as jnp
from jax import lax
from jax.experimental import pallas as pl
from jax.experimental.pallas import tpu as pltpu
from jax.sharding import PartitionSpec as P

highest = lax.Precision.HIGHEST
f32 = jnp.float32
vmem = pl.BlockSpec(memory_space=pltpu.VMEM)
hbm = pl.BlockSpec(memory_space=pl.ANY)
smem = pl.BlockSpec(memory_space=pltpu.SMEM)
params = pltpu.CompilerParams(vmem_limit_bytes=14 * 1024 * 1024)


def shape(*sizes):
    return jax.ShapeDtypeStruct(sizes, f32)


def dot(spec, left, right):
    return jnp.einsum(spec, left, right, precision=highest)


def product(left, right, dims):
    return lax.dot_general(left, right, (dims, ((), ())), precision=highest, preferred_element_type=f32)


def swap(x, axis):
    return lax.ppermute(x, axis, [(0, 1), (1, 0)])


def part(x, index):
    return lax.dynamic_index_in_dim(x, index, 0, keepdims=False)


def in_order(axis, mine, other):
    first = lax.axis_index(axis) == 0
    return jnp.stack([jnp.where(first, mine, other), jnp.where(first, other, mine)])


def trade(x, axis):
    if lax.axis_size(axis) != 2:
        return lax.all_to_all(x, axis, 0, 0, tiled=True)
    me = lax.axis_index(axis)
    return in_order(axis, part(x, me), swap(part(x, 1 - me), axis))


def gather(x, axis):
    if lax.axis_size(axis) != 2:
        return lax.all_gather(x, axis)
    return in_order(axis, x, swap(x, axis))


def total(x, axis):
    if lax.axis_size(axis) != 2:
        return lax.psum(x, axis)
    return x + swap(x, axis)


def mode_one(rows, core):
    a, s, t = rows.shape[0], core.shape[0], core.shape[1]
    halves = 128 // t
    q = s // halves

    def body(rows_ref, core_ref, out_ref):
        right = jnp.concatenate([core_ref[h * q + n] for n in range(q) for h in range(halves)], axis=0)
        both = product(rows_ref[...], right, ((1,), (1,)))
        for n in range(q):
            out_ref[:, n, :] = both[:, n * halves * t : (n + 1) * halves * t]

    return pl.pallas_call(
        body,
        out_shape=shape(a, q, halves * t),
        in_specs=[vmem, vmem],
        out_specs=vmem,
        compiler_params=params,
        cost_estimate=pl.CostEstimate(flops=12 * a * s * t * 128, bytes_accessed=4 * s * t * 128, transcendentals=0),
    )(rows, core)


def order_two(place, mine, other):
    ny, parts, half_j, wide = mine.shape

    def body(place_ref, mine_ref, other_ref, two_ref):
        me = place_ref[0]
        for c in range(parts):
            here = pl.ds(c * wide, wide)
            two_ref[:, pl.ds(me, 1), :, here] = mine_ref[:, c][:, None]
            two_ref[:, pl.ds(1 - me, 1), :, here] = other_ref[:, c][:, None]

    return pl.pallas_call(
        body,
        out_shape=shape(ny, 2, half_j, parts * wide),
        in_specs=[smem, vmem, vmem],
        out_specs=vmem,
        compiler_params=params,
    )(place, mine, other)


def mode_two(arrived, two, e, t):
    nz, ny, rows, wide = arrived.shape
    q, halves, half_j, full_s = rows // e, wide // t, two.shape[2], two.shape[3]
    j = nz * half_j

    def body(arrived_ref, two_ref, one_ref, moved_ref):
        for n in range(e):
            for h in range(halves):
                pieces = [arrived_ref[z, :, pl.ds(n * q, q), pl.ds(h * t, t)] for z in range(nz)]
                one_ref[:, h, :, pl.ds(n * wide, wide)] = jnp.concatenate(pieces, axis=-1)
        after = product(
            two_ref[...].reshape(ny * j, full_s), one_ref[...].reshape(full_s, e * wide), ((1,), (0,))
        )
        for n in range(e):
            moved_ref[:, n] = after[:, n * wide : (n + 1) * wide].reshape(ny, j, wide)

    return pl.pallas_call(
        body,
        out_shape=[shape(ny, halves, q, e * wide), shape(ny, e, j, wide)],
        in_specs=[vmem, vmem],
        out_specs=[vmem] * 2,
        compiler_params=params,
    )(arrived, two)


def back(place, moved, gram, gram_other, early, one, two):
    ny, e, j, wide = moved.shape
    _, halves, q, _ = one.shape
    _, nz, half_j, full_s = two.shape
    edge, parts = e * q, full_s // wide

    def body(place_ref, moved_ref, gram_ref, gram_other_ref, early_ref, one_ref, two_ref, keep_ref, send_ref, sum_ref, wide_ref):
        me = place_ref[0]
        square = gram_ref[...] + gram_other_ref[...]
        whole_two = two_ref[...].reshape(ny * j, full_s)
        for n in range(e):
            folded = product(moved_ref[:, n].reshape(ny * j, wide), square, ((1,), (0,)))
            folded = folded - early_ref[:, pl.ds(n * j, j)].reshape(ny * j, wide)
            term = product(folded, one_ref[:, :, :, pl.ds(n * wide, wide)].reshape(full_s, wide), ((1,), (1,)))
            term = term.reshape(ny, nz, half_j, full_s)
            if n == 0:
                sum_ref[...] = term
            else:
                sum_ref[...] += term
            spread = product(whole_two, folded, ((0,), (0,))).reshape(ny, halves, q, wide)
            for h in range(halves):
                wide_ref[h, :, pl.ds(n * q, q)] = spread[:, h]
        for ref, z in ((keep_ref, me), (send_ref, 1 - me)):
            ref[:, pl.ds(0, edge)] = wide_ref[pl.ds(z, 1)].reshape(ny, edge, wide)
            for c in range(parts):
                piece = sum_ref[:, pl.ds(z, 1), :, pl.ds(c * wide, wide)]
                ref[:, pl.ds(edge + c * half_j, half_j)] = piece.reshape(ny, half_j, wide)

    return pl.pallas_call(
        body,
        out_shape=[shape(ny, edge + parts * half_j, wide)] * 2,
        in_specs=[smem] + [vmem] * 6,
        out_specs=[vmem] * 2,
        scratch_shapes=[pltpu.VMEM((ny, nz, half_j, full_s), f32), pltpu.VMEM((halves, ny, edge, wide), f32)],
        compiler_params=params,
        cost_estimate=pl.CostEstimate(flops=10**9, bytes_accessed=2**21, transcendentals=0),
    )(place, moved, gram, gram_other, early, one, two)


def put(keep, arrived, edge, length):
    ny, rows, wide = keep.shape

    def body(keep_ref, arrived_ref, late_ref, both_ref, sems):
        copies = [
            pltpu.make_async_copy(ref.at[:, pl.ds(0, edge)], late_ref.at[:, pl.ds(n * edge, edge)], sems.at[n])
            for n, ref in enumerate((keep_ref, arrived_ref))
        ]
        for copy in copies:
            copy.start()
        at = pl.ds(edge, rows - edge)
        both_ref[...] = keep_ref[:, at] + arrived_ref[:, at]
        last = pltpu.make_async_copy(both_ref, late_ref.at[:, pl.ds(2 * edge, rows - edge)], sems.at[2])
        last.start()
        for copy in copies + [last]:
            copy.wait()

    return pl.pallas_call(
        body,
        out_shape=shape(ny, length, wide),
        in_specs=[vmem, vmem],
        out_specs=hbm,
        scratch_shapes=[pltpu.VMEM((ny, rows - edge, wide), f32), pltpu.SemaphoreType.DMA((3,))],
        compiler_params=params,
    )(keep, arrived)


def fit(half, field, after, factor_three, before=None):
    rows, k = field.shape
    block, full_t = after.shape
    pieces = 1

    def compute(half_ref, after_ref, factor_ref, residual_ref, field_ref, left_ref, sems):
        cut = block // pieces
        ats = [pl.ds(pl.multiple_of(half_ref[0] * block + n * cut, cut), cut) for n in range(pieces)]
        here = [pl.ds(n * cut, cut) for n in range(pieces)]
        loads = [pltpu.make_async_copy(residual_ref.at[ats[n]], field_ref.at[here[n]], sems.at[n]) for n in range(pieces)]
        outs = [pltpu.make_async_copy(left_ref.at[here[n]], residual_ref.at[ats[n]], sems.at[pieces + n]) for n in range(pieces)]
        for copy in loads:
            copy.start()
        after = after_ref[...]
        left = product(after, factor_ref[...].T, ((1,), (0,)))
        for copy in loads:
            copy.wait()
        left = left - field_ref[...]
        left_ref[...] = left
        for copy in outs:
            copy.start()
        return product(after, left, ((0,), (0,))), outs

    scratch = [pltpu.VMEM((block, k), f32), pltpu.VMEM((block, k), f32), pltpu.SemaphoreType.DMA((2 * pieces + 1,))]
    if before is None:

        def body(half_ref, _, after_ref, factor_ref, residual_ref, term_ref, field_ref, left_ref, sems):
            term, outs = compute(half_ref, after_ref, factor_ref, residual_ref, field_ref, left_ref, sems)
            term_ref[...] = term
            for copy in outs:
                copy.wait()

        return pl.pallas_call(
            body,
            out_shape=[shape(rows, k), shape(full_t, k)],
            in_specs=[smem, hbm, vmem, vmem],
            out_specs=[hbm, vmem],
            scratch_shapes=scratch,
            input_output_aliases={1: 0},
            compiler_params=params,
        )(half, field, after, factor_three)

    term, late = before
    ny, length, _ = late.shape
    cut = k // ny

    def body(half_ref, _, after_ref, factor_ref, term_ref, __, residual_ref, late_ref, field_ref, left_ref, sems, parted_ref):
        term, outs = compute(half_ref, after_ref, factor_ref, residual_ref, field_ref, left_ref, sems)
        parted_ref[...] = (term + term_ref[...]).T.reshape(ny, cut, full_t)
        message = pltpu.make_async_copy(parted_ref, late_ref.at[:, pl.ds(length - cut, cut)], sems.at[2 * pieces])
        message.start()
        for copy in outs:
            copy.wait()
        message.wait()

    return pl.pallas_call(
        body,
        out_shape=[shape(rows, k), shape(*late.shape)],
        in_specs=[smem, hbm, vmem, vmem, vmem, hbm],
        out_specs=[hbm, hbm],
        scratch_shapes=scratch + [pltpu.VMEM((ny, cut, full_t), f32)],
        input_output_aliases={1: 0, 5: 1},
        compiler_params=params,
    )(half, field, after, factor_three, term, late)


def mode_one_term(place, late, own_mine, own_other, near_mine, near_other, e):
    ny, _, wide = late.shape
    q, t, r = own_mine.shape
    edge, half = e * q, ny * e * q
    i = 2 * ny * e
    group = min(q, 256 // t)

    def body(place_ref, late_ref, own_mine_ref, own_other_ref, near_mine_ref, near_other_ref, keep_ref, send_ref, rows_ref):
        for n, z in enumerate((place_ref[0], 1 - place_ref[0])):
            rows_ref[pl.ds(pl.multiple_of(z * half, half), half), :] = late_ref[:, pl.ds(n * edge, edge)].reshape(half, wide)
        first = place_ref[0] == 0
        sum_here = jnp.zeros((i, 2 * r), f32)
        for p in range(0, q, group):
            parts = [rows_ref[pl.ds(p + m, i, stride=q), :] for m in range(group)]
            low = jnp.concatenate([x[:, :t] for x in parts], axis=1)
            high = jnp.concatenate([x[:, t:] for x in parts], axis=1)
            for left, pair in (
                (jnp.where(first, low, high), (own_mine_ref, near_mine_ref)),
                (jnp.where(first, high, low), (own_other_ref, near_other_ref)),
            ):
                right = jnp.concatenate([ref[pl.ds(p, group)].reshape(group * t, r) for ref in pair], axis=1)
                sum_here = sum_here + product(left, right, ((1,), (0,)))
        same = place_ref[0] == place_ref[1]
        keep_ref[...] = jnp.where(same, sum_here[:, :r], sum_here[:, r:])
        send_ref[...] = jnp.where(same, sum_here[:, r:], sum_here[:, :r])

    return pl.pallas_call(
        body,
        out_shape=[shape(i, r), shape(i, r)],
        in_specs=[smem] + [vmem] * 5,
        out_specs=[vmem] * 2,
        scratch_shapes=[pltpu.VMEM((i * q, wide), f32)],
        compiler_params=params,
    )(place, late, own_mine, own_other, near_mine, near_other)


def local(tensor, core, factor_one, factor_two, factor_three):
    nx, ny, nz = lax.axis_size("gx"), lax.axis_size("gy"), lax.axis_size("gz")
    i, j, k = tensor.shape
    r, s, t = core.shape
    e, q, full_t, full_s, full_r = i // (ny * nz), s // nz, t * nz, s * ny, r * nx
    half_j, half_r, rows = j // nz, full_r // nz, i * j
    gx, gz = lax.axis_index("gx"), lax.axis_index("gz")
    place = jnp.stack([gz, gx]).astype(jnp.int32)
    flat = core.transpose(1, 2, 0)

    if nx == 2:
        other_one = swap(lax.dynamic_slice_in_dim(factor_one, (1 - gx) * r, r, axis=1), "gx")

    half = place[:1]
    field = tensor.reshape(rows, k)
    halves = tensor.reshape(nz, rows // nz, k)
    folded = swap(dot("ac,ct->at", part(halves, 1 - gz), factor_three), "gz")
    folded = folded + dot("ac,ct->at", part(halves, gz), factor_three)
    mine_two = part(factor_two.reshape(nz, half_j, full_s), gz)
    mine_two = jnp.concatenate([mine_two[:, c * full_t : (c + 1) * full_t] for c in range(full_s // full_t)], axis=0)
    early = jnp.concatenate(
        [folded.reshape(ny, e * j, full_t), jnp.broadcast_to(mine_two[None], (ny,) + mine_two.shape)], axis=1
    )
    if nx == 2:
        mine_one = lax.dynamic_slice_in_dim(factor_one, gx * r, r, axis=1)
        early, other_one = lax.optimization_barrier((early, other_one))
        sent = swap(mode_one(other_one, flat), "gx")
        after_one = mode_one(mine_one, flat) + sent
    else:
        every_one = trade(factor_one.reshape(i, nx, r).transpose(1, 0, 2), "gx")
        after_one = dot("xar,hqtr->xaqht", every_one, flat.reshape(nz, q, t, r)).reshape(nx, i, q, full_t)
        after_one = lax.psum_scatter(after_one, "gx", scatter_dimension=0)

    early = lax.all_to_all(early, "gy", 0, 0, tiled=True)
    early, after_one = lax.optimization_barrier((early, after_one))
    mine_two = early[:, e * j :].reshape(ny, full_s // full_t, half_j, full_t)
    other_two = swap(mine_two, "gz")
    gram = dot("ct,cu->tu", factor_three, factor_three)
    gram_other = swap(gram, "gz")

    flat = flat.reshape(nz, q, t, r)
    if nx == 2:
        own_mine, own_other = part(flat, gz), swap(part(flat, 1 - gz), "gz")
        near_mine = swap(own_mine, "gx")
    after_one = lax.all_to_all(after_one.reshape(nz * ny, e * q, full_t), ("gz", "gy"), 0, 0, tiled=True)
    two = order_two(place, mine_two, other_two)
    after_one, gram_other, two = lax.optimization_barrier((after_one, gram_other, two))
    after_one = after_one.reshape(nz, ny, e * q, full_t)
    one, moved = mode_two(after_one, two, e, t)
    home = lax.all_to_all(moved, "gy", 0, 0, tiled=True).reshape(rows // nz, full_t)
    edge, parts = e * q, full_s // full_t
    keep, send = back(place, moved, gram, gram_other, early, one, two)
    late = put(keep, swap(send, "gz"), edge, 2 * edge + parts * half_j + k // ny)
    if nx == 2:
        home, late, near_mine = lax.optimization_barrier((home, late, near_mine))
    field, term_three = fit(half, field, home, factor_three)
    residual, late = fit(1 - half, field, swap(home, "gz"), factor_three, (term_three, late))
    if nx == 2:
        late, own_other = lax.optimization_barrier((late, own_other))
    late = lax.all_to_all(late, "gy", 0, 0, tiled=True)
    sums = total(late[:, 2 * edge :].sum(axis=0), "gx")
    share_two, share_three = sums[: parts * half_j], sums[parts * half_j :]
    if nx == 2:
        keep_one, send_one = mode_one_term(place, late, own_mine, own_other, near_mine, swap(own_other, "gx"), e)
        term_one = keep_one + swap(send_one, "gz")
    else:
        share_one = in_order("gz", late[:, :edge], late[:, edge : 2 * edge]).reshape(i, q, full_t)
        every_core = gather(trade(flat, "gz"), "gx")
        term_one = dot("aqht,xhqtr->axr", share_one.reshape(i, q, nz, t), every_core)
        term_one = lax.psum_scatter(term_one.reshape(i, nz, half_r).transpose(1, 0, 2), "gz", scatter_dimension=0)

    last = jnp.concatenate([term_one.reshape(-1, full_t), share_three], axis=0)
    last = lax.all_to_all(jnp.broadcast_to(last[None], (ny,) + last.shape), "gy", 0, 0, tiled=True)
    share_two = jnp.concatenate([share_two[c * half_j : (c + 1) * half_j] for c in range(parts)], axis=1)
    grad_two = gather(share_two, "gz").reshape(j, full_s) / jnp.sqrt(f32(i * nx * k * nz))
    last, grad_two = lax.optimization_barrier((last, grad_two))

    cut = i * half_r // full_t
    grad_one = gather(last[:, :cut].sum(axis=0).reshape(i, half_r), "gz")
    grad_one = jnp.concatenate([grad_one[z] for z in range(nz)], axis=1) / jnp.sqrt(f32(j * ny * k * nz))
    grad_three = last[:, cut:].reshape(k, full_t) / jnp.sqrt(f32(i * nx * j * ny))
    return (residual.reshape(i, j, k), grad_one, grad_two, grad_three)


def solution(mesh):
    placed = (P("gx", "gy", "gz"), P("gx", "gy", "gz"), P("gx", None), P("gy", None), P("gz", None))
    return jax.shard_map(
        local,
        mesh=mesh,
        in_specs=placed,
        out_specs=(P("gx", "gy", "gz"), P("gx", None), P("gy", None), P("gz", None)),
        check_vma=False,
    )
```
